32 devices in a mesh: pool: 4 (over x, core), dev: 8 (over z, y).
Axes of the slice: x: 2, y: 2, z: 4, core: 2. Of those that a mesh axis runs over, the one named last changes fastest.
Arguments:
- hidden_in: bfloat16 [32, 7168], P('pool', 'dev'), may hold values from -32 to 32
- in_gain: float32 [7168], P('dev'), may hold values from 0.25 to 1.75
- w_latent: bfloat16 [7168, 2560], P('dev'), may hold values from -0.0625 to 0.0625
- q_gain: float32 [2048], replicated, may hold values from 0.25 to 1.75
- w_query: bfloat16 [2048, 16384], P(None, 'dev'), may hold values from -0.125 to 0.125
- cache_keys: bfloat16 [32, 4096, 256], P('pool', 'dev'), may hold values from -240 to 240
- cache_values: bfloat16 [32, 4096, 256], P('pool', 'dev'), may hold values from -6 to 6
- lengths: int32 [32], P('pool'), may hold values from 1 to 4096, 65536 in all
- w_out: bfloat16 [16384, 7168], P('dev'), may hold values from -0.125 to 0.125
- post_gain: float32 [7168], P('dev'), may hold values from 0.25 to 1.75
- w_gate: bfloat16 [7168, 18432], P(None, ('pool', 'dev')), may hold values from -0.0625 to 0.0625
- w_up: bfloat16 [7168, 18432], P(None, ('pool', 'dev')), may hold values from -0.0625 to 0.0625
- w_down: bfloat16 [18432, 7168], P(('pool', 'dev')), may hold values from -0.078125 to 0.078125
Outputs:
- mixed: float32 [32, 7168], P('pool', 'dev')
The draws below stay inside these ranges and needn't reach their ends.
All inputs are finite; a program needn't handle non-finite values. No bound on the sum of `lengths` on one device may be relied on, other than what follows from the above.
Results may differ from the reference program's by a relative error of at most 0.013.
Values may be sent and summed in bfloat16 or wider, within the bound.
No kernel may reach another device: no remote copies, remote signals or barrier semaphores. Data moves between devices by JAX's collectives and lax.ppermute only.
A program may use at most 128 MiB of HBM per device.

```python
import math
import jax
import jax.numpy as jnp
import numpy as np
from jax import lax

D = 7168
H = 64
HD = 256
QR = 2048
FF = 18432
ROWS = 32
CACHE = 4096


def draw_hidden_in(key, part):
    key = jax.random.fold_in(key, 1)
    row_key, col_key, field_key = jax.random.split(key, 3)
    row_scale = jnp.exp(jax.random.uniform(row_key, (ROWS, 1), jnp.float32, math.log(0.4), math.log(2.5)))
    col_spread = jnp.exp(jax.random.uniform(col_key, (1, D), jnp.float32, math.log(0.75), math.log(1.33)))
    ramp = jnp.arange(D, dtype=jnp.float32)[None, :] / (D - 1)
    col_scale = jnp.exp(math.log(0.5) + math.log(10.0) * ramp) * col_spread
    base_field = jnp.clip(jax.random.normal(field_key, (ROWS, D), jnp.float32), -4.0, 4.0)
    return jnp.clip(base_field * row_scale * col_scale, -32.0, 32.0).astype(jnp.bfloat16)


def draw_cache_keys(key, part):
    key = jax.random.fold_in(key, 2)
    base_field = jnp.clip(jax.random.normal(key, (ROWS, CACHE, HD), jnp.float32), -4.0, 4.0)
    return base_field.astype(jnp.bfloat16)


def strengthened(drawn, key, source, target, parts, factor):
    def block_of(position):
        return (jnp.arange(drawn.shape[position]) // (drawn.shape[position] // parts)).reshape((-1,) + (1,) * (drawn.ndim - 1 - position))

    near = jax.random.permutation(key, parts)[block_of(target)]
    second = (block_of(target) + parts // 2) % parts
    return jnp.where((block_of(source) == near) | (block_of(source) == second), factor * drawn, drawn)


def block_scale(rng, dims, cuts, least, largest):
    def one(dim, blocks):
        heights = jax.random.uniform(jax.random.fold_in(jax.random.fold_in(rng, 6), dim), (blocks,), jnp.float32, least / len(cuts), largest / len(cuts))
        return jnp.repeat(jnp.exp(heights), dims[dim] // blocks).reshape((-1,) + (1,) * (len(dims) - dim - 1))

    factor_of = one(*cuts[0])
    for cut in cuts[1:]:
        factor_of = factor_of * one(*cut)
    return factor_of


def split_up(count, total, limit, skew):
    loads = [(1 << 20) // math.isqrt(rank ** skew) + 1 for rank in range(2, count + 1)]
    surplus, given = total - limit - (count - 1), [1] * (count - 1)
    while surplus > 0:
        free = [i for i in range(count - 1) if given[i] < limit]
        whole, budget = sum([loads[i] for i in free]), surplus
        for i in free:
            extra = min(limit - given[i], max(1, budget * loads[i] // whole), surplus)
            given[i] = given[i] + extra
            surplus = surplus - extra
    return np.array([limit] + given)


def ragged(key, number_of, total, reach, slope):
    if number_of == 2:
        one = jax.random.randint(key, (), max(1, total - reach), min(reach, total - 1) + 1)
        return jnp.stack([one, total - one])
    sizes = jnp.asarray(split_up(number_of, total, reach, slope), jnp.int32)
    pairs = (number_of - 1) // 2
    giver, taker = sizes[1:1 + 2 * pairs:2], sizes[2:2 + 2 * pairs:2]
    margin = jnp.minimum(giver - 1, reach - taker)
    passed = jax.random.randint(jax.random.fold_in(key, 1), (pairs,), 0, 1 << 20) % (margin + 1)
    sizes = sizes.at[1:1 + 2 * pairs:2].set(giver - passed).at[2:2 + 2 * pairs:2].set(taker + passed)
    return sizes[jax.random.permutation(jax.random.fold_in(key, 2), number_of)]


def noise(own_key, extent, spread, reach, shards=(), held_as=jnp.bfloat16):
    entries = jax.random.normal(own_key, extent, jnp.float32) * spread
    if len(shards) > 0:
        entries = block_scale(own_key, extent, shards, -0.22, 0.18) * entries
    return jnp.clip(entries, min=-reach, max=reach).astype(held_as)


def noise_with(stream_key, dims, scale, reach, cuts, heavy, kind=jnp.bfloat16):
    result = scale * jax.random.normal(stream_key, dims, jnp.float32)
    if cuts:
        result = result * block_scale(stream_key, dims, cuts, -0.22, 0.18)
    return jnp.clip(strengthened(result, jax.random.fold_in(stream_key, 3), *heavy), -reach, reach).astype(kind)


def setup_inputs(seed: int = 0) -> dict:
    streams_of = jax.random.split(jax.random.key(seed), 14)
    hidden_in = draw_hidden_in(jax.random.fold_in(streams_of[13], 71), 0)
    in_gain = jnp.clip(1.0 + 0.15 * jax.random.normal(streams_of[1], (D,), jnp.float32), 0.25, 1.75)
    w_latent = noise(streams_of[2], (D, QR + 2 * HD), D ** -0.5, 0.0625, ((0, 8),))
    q_gain = jnp.clip(1.0 + 0.15 * jax.random.normal(streams_of[3], (QR,), jnp.float32), 0.25, 1.75)
    w_query = noise(streams_of[4], (QR, H * HD), QR ** -0.5, 0.125, ((1, 8),))
    cache_keys = draw_cache_keys(jax.random.fold_in(streams_of[13], 71), 0)
    cache_values = noise(streams_of[6], (ROWS, CACHE, HD), 1.0, 6.0, ((0, 4), (1, 8)))
    lengths = ragged(streams_of[7], ROWS, ROWS * CACHE // 2, CACHE, 2).astype(jnp.int32)
    w_out = noise_with(streams_of[8], (H * HD, D), (H * HD // 4) ** -0.5, 0.125, ((0, 8),), (0, 1, 8, 2.0))
    post_gain = jnp.clip(1.0 + 0.15 * jax.random.normal(streams_of[9], (D,), jnp.float32), 0.25, 1.75)
    w_gate = noise(streams_of[10], (D, FF), D ** -0.5, 0.0625, ((1, 32),))
    w_up = noise(streams_of[11], (D, FF), D ** -0.5, 0.0625, ((1, 32),))
    w_down = noise_with(streams_of[12], (FF, D), FF ** -0.5, 0.078125, ((0, 32),), (0, 1, 32, 2.75))
    return dict(hidden_in=hidden_in, in_gain=in_gain, w_latent=w_latent, q_gain=q_gain, w_query=w_query, cache_keys=cache_keys, cache_values=cache_values, lengths=lengths, w_out=w_out, post_gain=post_gain, w_gate=w_gate, w_up=w_up, w_down=w_down)


EPS = 1e-05
NEG = -1e+30

def attend_block(items):
    query, keys, values, key_new, value_new, length = items
    scale_inv = 1.0 / math.sqrt(HD)
    query_f = query.astype(jnp.float32)
    scores = jnp.einsum('bhd,bpd->bhp', query_f, keys.astype(jnp.float32)) * scale_inv
    fresh = lax.optimization_barrier(jnp.sum(query_f * key_new.astype(jnp.float32)[:, None, :], axis=-1)) * scale_inv
    positions = jnp.arange(CACHE, dtype=jnp.int32)
    valid_mask = (positions[None, :] < length[:, None])[:, None, :]
    masked = jnp.where(valid_mask, scores, NEG)
    highest = jnp.maximum(lax.optimization_barrier(jnp.max(masked, axis=-1)), fresh)
    weights = jnp.where(valid_mask, jnp.exp(masked - highest[..., None]), 0.0)
    fresh_weight = jnp.exp(fresh - highest)
    mass = lax.optimization_barrier(jnp.sum(weights, axis=-1)) + fresh_weight
    rounded = weights.astype(jnp.bfloat16).astype(jnp.float32)
    numerator = jnp.einsum('bhp,bpd->bhd', rounded, values.astype(jnp.float32))
    numerator = numerator + fresh_weight.astype(jnp.bfloat16).astype(jnp.float32)[..., None] * value_new.astype(jnp.float32)[:, None, :]
    return (numerator / mass[..., None]).astype(jnp.bfloat16)

def reference(hidden_in, in_gain, w_latent, q_gain, w_query, cache_keys, cache_values, lengths, w_out, post_gain, w_gate, w_up, w_down):
    hidden_f = hidden_in.astype(jnp.float32)
    row_mean = lax.optimization_barrier(jnp.mean(hidden_f * hidden_f, axis=1))
    scaled_in = (hidden_f * in_gain[None, :]).astype(jnp.bfloat16)
    latent = jnp.dot(scaled_in, w_latent, preferred_element_type=jnp.float32) * lax.rsqrt(row_mean + EPS)[:, None]
    query_latent = latent[:, :QR]
    key_new = latent[:, QR:QR + HD].astype(jnp.bfloat16)
    value_new = latent[:, QR + HD:].astype(jnp.bfloat16)
    latent_mean = lax.optimization_barrier(jnp.mean(query_latent * query_latent, axis=1))
    query_normed = (query_latent * lax.rsqrt(latent_mean + EPS)[:, None] * q_gain[None, :]).astype(jnp.bfloat16)
    query = jnp.dot(query_normed, w_query, preferred_element_type=jnp.float32).astype(jnp.bfloat16)
    blocks = ROWS // 8
    attended = lax.map(attend_block, (query.reshape(blocks, 8, H, HD), cache_keys.reshape(blocks, 8, CACHE, HD), cache_values.reshape(blocks, 8, CACHE, HD), key_new.reshape(blocks, 8, HD), value_new.reshape(blocks, 8, HD), lengths.reshape(blocks, 8)))
    attended = attended.reshape(ROWS, H * HD)
    residual = hidden_f + jnp.dot(attended, w_out, preferred_element_type=jnp.float32)
    res_mean = lax.optimization_barrier(jnp.mean(residual * residual, axis=1))
    normed = (residual * lax.rsqrt(res_mean + EPS)[:, None] * post_gain[None, :]).astype(jnp.bfloat16)
    gate_out = jnp.dot(normed, w_gate, preferred_element_type=jnp.float32)
    up_out = jnp.dot(normed, w_up, preferred_element_type=jnp.float32)
    activated = (jax.nn.silu(gate_out) * up_out).astype(jnp.bfloat16)
    return residual + jnp.dot(activated, w_down, preferred_element_type=jnp.float32)
```

```python
import functools
import math

import jax
import jax.numpy as jnp
from jax import lax
from jax.experimental import pallas as pl
from jax.experimental.pallas import tpu as pltpu
from jax.sharding import PartitionSpec as P

D = 7168
H = 64
HD = 256
QR = 2048
LATENT = QR + 2 * HD
LANES = 128
STATS = 16

EPS = 1e-05
NEG = -1e30

FAR, CORE, DEV = "far", "core", "dev"
POOL = (FAR, CORE)
F32, BF16 = jnp.float32, jnp.bfloat16
MIB = 1 << 20
VMEM = pl.BlockSpec(memory_space=pltpu.VMEM)
HBM = pl.BlockSpec(memory_space=pltpu.MemorySpace.HBM)


def dot(left, right, left_dim=1, right_dim=0):
    return lax.dot_general(
        left,
        right,
        (((left_dim,), (right_dim,)), ((), ())),
        preferred_element_type=F32,
    )


def whole(shape):
    return pl.BlockSpec(shape, lambda *_: (0,) * len(shape))


def params(mib):
    return pltpu.CompilerParams(vmem_limit_bytes=mib * MIB)


def streamed(weight):
    return pltpu.with_memory_space_constraint(weight, pltpu.MemorySpace.HBM)


def cost(flops, moved):
    return pl.CostEstimate(flops=flops, bytes_accessed=moved, transcendentals=0)


def started(source, target, sems, pieces, axis):
    width = source.shape[axis] // pieces
    copies = []
    for piece in range(pieces):
        span = pl.ds(piece * width, width)
        at = (slice(None),) * axis + (span,)
        copy = pltpu.make_async_copy(source.at[at], target.at[at], sems.at[piece])
        copy.start()
        copies.append(copy)
    return copies


def ahead_kernel(count, *refs):
    sources, targets = refs[1 : 1 + count], refs[1 + count : 1 + 2 * count]
    token_ref, sems = refs[-2:]
    copies = []
    for index, (source, target) in enumerate(zip(sources, targets)):
        copies.append(pltpu.make_async_copy(source.at[...], target, sems.at[index]))
        copies[-1].start()
    token_ref[...] = jnp.zeros_like(token_ref)
    for copy in copies:
        copy.wait()


def ahead(beside, weights):
    count = len(weights)
    shapes = [w.shape for w in weights]
    *copied, token = pl.pallas_call(
        functools.partial(ahead_kernel, count),
        in_specs=[pl.BlockSpec(memory_space=pl.ANY)] + [HBM] * count,
        out_specs=[VMEM] * (count + 1),
        out_shape=[pltpu.VMEM(shape, BF16) for shape in shapes]
        + [jax.ShapeDtypeStruct((8, LANES), F32)],
        scratch_shapes=[pltpu.SemaphoreType.DMA((count,))],
        compiler_params=params(1),
        cost_estimate=cost(0, sum(2 * math.prod(shape) for shape in shapes)),
    )(beside, *[streamed(w) for w in weights])
    return copied, token


def part_ahead(beside, weight, part, parts, height, held):
    def kernel(*refs):
        source, (target, token_ref, sem) = refs[1], refs[-3:]
        rows = pl.ds(part * height, height)
        copy = pltpu.make_async_copy(source.at[rows], target.at[rows], sem)
        copy.start()
        token_ref[...] = jnp.zeros_like(token_ref)
        copy.wait()

    buffers = [] if held is None else [held]
    return pl.pallas_call(
        kernel,
        in_specs=[pl.BlockSpec(memory_space=pl.ANY), HBM] + [VMEM] * len(buffers),
        out_specs=[VMEM] * 2,
        out_shape=[
            pltpu.VMEM((parts * height, weight.shape[1]), BF16),
            jax.ShapeDtypeStruct((8, LANES), F32),
        ],
        scratch_shapes=[pltpu.SemaphoreType.DMA],
        input_output_aliases={2: 0} if buffers else {},
        compiler_params=params(1),
        cost_estimate=cost(0, 2 * height * weight.shape[1]),
    )(beside, streamed(weight), *buffers)


def joined(left, right, token, add):
    def kernel(left_ref, right_ref, token_ref, out_ref):
        if add:
            out_ref[...] = left_ref[...] + right_ref[...]
        else:
            both = [left_ref[...].astype(F32), right_ref[...].astype(F32)]
            out_ref[...] = jnp.concatenate(both, axis=0).astype(out_ref.dtype)

    rows, cols = left.shape
    return pl.pallas_call(
        kernel,
        in_specs=[VMEM] * 3,
        out_specs=VMEM,
        out_shape=jax.ShapeDtypeStruct((rows if add else 2 * rows, cols), left.dtype),
        compiler_params=params(2),
        cost_estimate=cost(0, 3 * rows * cols * left.dtype.itemsize),
    )(left, right, token)


def query_kernel(left_ref, right_ref, token_ref, gain_ref, w_ref, query_ref, fresh_ref, wide_ref):
    sums_ref = left_ref[...] + right_ref[...]
    rows = sums_ref.shape[0]
    out = w_ref.shape[1]
    width = min(512, out)
    heads = query_ref.shape[0] // rows
    factor = lax.rsqrt(sums_ref[:, LATENT : LATENT + 1] / D + EPS)
    query_latent = sums_ref[:, :QR] * factor
    mean = jnp.sum(query_latent * query_latent, axis=1, keepdims=True) / QR
    normed = (query_latent * lax.rsqrt(mean + EPS) * gain_ref[...]).astype(BF16)
    fresh = sums_ref[:, QR:LATENT] * factor
    fresh_ref[...] = fresh.astype(BF16).astype(F32)
    for step in range(out // width):
        query = dot(normed, w_ref[:, step * width : (step + 1) * width])
        for part in range(width // HD):
            head = step * (width // HD) + part
            for row in range(rows):
                wide_ref[row * heads + head : row * heads + head + 1, :] = query[
                    row : row + 1, part * HD : (part + 1) * HD
                ]
    query_ref[...] = wide_ref[...].astype(BF16)


def queries(left, right, token, gain, w):
    rows = left.shape[0]
    out = w.shape[1]
    heads = out // HD
    return pl.pallas_call(
        query_kernel,
        in_specs=[VMEM] * 5,
        out_specs=[VMEM] * 2,
        out_shape=[
            jax.ShapeDtypeStruct((rows * heads, HD), BF16),
            jax.ShapeDtypeStruct((rows, 2 * HD), F32),
        ],
        scratch_shapes=[pltpu.VMEM((rows * heads, HD), F32)],
        compiler_params=params(2),
        cost_estimate=cost(2 * rows * QR * out, 2 * QR * out),
    )(left, right, token, gain.reshape(1, QR), w)


def attend_kernel(codes, place_ref, lengths_ref, token_ref, *refs):
    n_dev = len(codes)
    pieces, refs = refs[:-6], refs[-6:]
    keys_ref, values_ref, out_ref, wide_ref, parts_ref, weights_ref = refs
    rows, local_pos = keys_ref.shape[:2]
    heads = H // n_dev
    me = place_ref[0]
    at = 0
    for piece in pieces:
        size = piece.shape[0]
        wide_ref[at : at + size, :] = piece[...].astype(F32)
        at += size
    lane = lax.broadcasted_iota(jnp.int32, (H, LANES), 1)
    columns = lax.broadcasted_iota(jnp.int32, (H, local_pos), 1) + me * local_pos
    stats = jnp.zeros((H, LANES), F32)
    for row in range(rows):
        query = jnp.concatenate(
            [
                wide_ref[(g * rows + row) * heads : (g * rows + row + 1) * heads, :]
                for g in range(n_dev)
            ],
            axis=0,
        ).astype(BF16)
        scores = dot(query, keys_ref[row], 1, 1) * (1.0 / math.sqrt(HD))
        valid = columns < lengths_ref[row]
        masked = jnp.where(valid, scores, NEG)
        top = jnp.max(masked, axis=1, keepdims=True)
        weights = jnp.where(valid, jnp.exp(masked - top), 0.0)
        mass = jnp.sum(weights, axis=1, keepdims=True)
        weights_ref[row] = weights.astype(BF16)
        stats = jnp.where(lane == row, top, stats)
        stats = jnp.where(lane == rows + row, mass, stats)
    for row in range(rows):
        weighted = dot(weights_ref[row], values_ref[row])
        for g in range(n_dev):
            parts_ref[me ^ codes[g], row * heads : (row + 1) * heads, :] = weighted[
                g * heads : (g + 1) * heads, :
            ]
    high = stats.astype(BF16).astype(F32)
    rest = stats - high
    middle = rest.astype(BF16).astype(F32)
    low = rest - middle
    at = rows * heads
    parts_ref[:, at:, :] = jnp.zeros((n_dev, STATS, HD), F32)
    for g in range(n_dev):
        span = slice(g * heads, (g + 1) * heads)
        parts_ref[me ^ codes[g], at : at + heads, :LANES] = high[span]
        parts_ref[me ^ codes[g], at : at + heads, LANES:] = middle[span]
        parts_ref[me ^ codes[g], at + 8 : at + 8 + heads, :LANES] = low[span]
    out_ref[...] = parts_ref[...].astype(BF16)


def attend(codes, place, lengths, token, pieces, keys, values):
    rows, local_pos = keys.shape[:2]
    n_dev = len(codes)
    height = rows * H // n_dev + STATS
    smem = pl.BlockSpec(memory_space=pltpu.SMEM)
    return pl.pallas_call(
        functools.partial(attend_kernel, codes),
        in_specs=[smem, smem] + [VMEM] * (3 + len(pieces)),
        out_specs=VMEM,
        out_shape=jax.ShapeDtypeStruct((n_dev, height, HD), BF16),
        scratch_shapes=[
            pltpu.VMEM((rows * H, HD), F32),
            pltpu.VMEM((n_dev, height, HD), F32),
            pltpu.VMEM((rows, H, local_pos), BF16),
        ],
        compiler_params=params(5),
        cost_estimate=cost(4 * rows * H * local_pos * HD, 4 * rows * local_pos * HD),
    )(place, lengths, token, *pieces, keys, values)


def project_kernel(
    sent_ref, query_ref, fresh_ref, held_ref, w_hbm, out_ref, attended_ref, parts_ref, w_ref, sems
):
    n_dev = sent_ref.shape[0]
    held = held_ref.shape[0]
    copies = started(w_hbm.at[held : held + w_ref.shape[0]], w_ref, sems, out_ref.shape[0], 1)
    rows = fresh_ref.shape[0]
    heads = H // n_dev

    query = query_ref[...].astype(F32)
    parts_ref[...] = sent_ref[...].astype(F32)
    at = rows * heads
    stats = [
        parts_ref[d, at : at + heads, :LANES]
        + parts_ref[d, at : at + heads, LANES:]
        + parts_ref[d, at + 8 : at + 8 + heads, :LANES]
        for d in range(n_dev)
    ]
    for row in range(rows):
        span = slice(row * heads, (row + 1) * heads)
        key = fresh_ref[row : row + 1, :HD]
        value = fresh_ref[row : row + 1, HD:]
        score = jnp.sum(query[span] * key, axis=1, keepdims=True) * (1.0 / math.sqrt(HD))
        highest = score
        for d in range(n_dev):
            highest = jnp.maximum(highest, stats[d][:, row : row + 1])
        weight = jnp.exp(score - highest)
        mass = weight
        total = weight.astype(BF16).astype(F32) * value
        for d in range(n_dev):
            factor = jnp.exp(stats[d][:, row : row + 1] - highest)
            mass = mass + factor * stats[d][:, rows + row : rows + row + 1]
            total = total + factor * parts_ref[d, span, :]
        attended = total / mass
        for head in range(heads):
            attended_ref[row : row + 1, head * HD : (head + 1) * HD] = attended[
                head : head + 1, :
            ]

    width = out_ref.shape[2]
    attended = attended_ref[...].astype(BF16)
    for step, copy in enumerate(copies):
        columns = slice(step * width, (step + 1) * width)
        first = dot(attended[:, :held], held_ref[:, columns])
        copy.wait()
        out_ref[step] = first + dot(attended[:, held:], w_ref[:, columns])


def project(parts, query, fresh, held, w):
    rows = fresh.shape[0]
    depth = w.shape[0]
    width = D // 8
    return pl.pallas_call(
        project_kernel,
        in_specs=[VMEM] * 4 + [HBM],
        out_specs=VMEM,
        out_shape=jax.ShapeDtypeStruct((D // width, rows, width), F32),
        scratch_shapes=[
            pltpu.VMEM((rows, depth), F32),
            pltpu.VMEM(parts.shape, F32),
            pltpu.VMEM((depth - held.shape[0], D), BF16),
            pltpu.SemaphoreType.DMA((D // width,)),
        ],
        compiler_params=params(20),
        cost_estimate=cost(2 * rows * depth * D, 2 * depth * D),
    )(parts, query, fresh, held, streamed(w))


def ffn_kernel(*refs):
    pieces, refs = refs[:-6], refs[-6:]
    token_ref, gate_ref, up_ref, down_ref, out_ref, act_ref = refs
    rows = jnp.concatenate([piece[...] for piece in pieces], axis=0)
    units = gate_ref.shape[0]
    block = 144
    for step in range(units // block):
        span = slice(step * block, (step + 1) * block)
        gate = dot(gate_ref[span, :], rows, 1, 1)
        up = dot(up_ref[span, :], rows, 1, 1)
        act_ref[span, :] = gate / (1.0 + jnp.exp(-gate)) * up
    activated = act_ref[...].astype(BF16)
    width = down_ref.shape[1] // 8

    @pl.loop(0, 8)
    def _(step):
        columns = pl.ds(pl.multiple_of(step * width, width), width)
        out_ref[:, columns] = dot(activated, down_ref[:, columns], 0, 0)


def ffn(pieces, token, gate_t, up_t, down):
    rows = sum(piece.shape[0] for piece in pieces)
    units, depth = gate_t.shape
    return pl.pallas_call(
        ffn_kernel,
        in_specs=[VMEM] * (len(pieces) + 4),
        out_specs=VMEM,
        out_shape=jax.ShapeDtypeStruct((rows, depth), F32),
        scratch_shapes=[pltpu.VMEM((units, rows), F32)],
        compiler_params=params(6),
        cost_estimate=cost(6 * rows * units * depth, 6 * units * depth),
    )(*pieces, token, gate_t, up_t, down)


def swapped(value, axis, bit):
    size = lax.axis_size(axis)
    return lax.ppermute(value, axis, [(i, i ^ bit) for i in range(size)])


def gathered(value, axis):
    size = lax.axis_size(axis)
    return lax.all_to_all(jnp.broadcast_to(value[None], (size, *value.shape)), axis, 0, 0)


def local(
    hidden_in,
    in_gain,
    w_latent,
    q_gain,
    w_query,
    cache_keys,
    cache_values,
    lengths,
    w_out,
    post_gain,
    w_gate,
    w_up,
    w_down,
):
    n_dev = lax.axis_size(DEV)
    place = lax.axis_index(DEV).astype(jnp.int32).reshape(1)
    rows, cols = hidden_in.shape
    hidden_f = hidden_in.astype(F32)

    scaled = (hidden_f * in_gain[None, :]).astype(BF16)
    squares = jnp.sum(hidden_f * hidden_f, axis=1, keepdims=True)
    sums = jnp.concatenate(
        [dot(scaled, w_latent), jnp.broadcast_to(squares, (rows, LANES))], axis=1
    )
    copied = {}

    def copy_query(value):
        (copied["query"],), token = ahead(value, [w_query])
        return token

    def copy_out(part, value):
        height = w_out.shape[0] // 8
        copied["out"], token = part_ahead(value, w_out, part, 4, height, copied.get("out"))
        return token

    def copy_caches(value):
        copied["caches"], token = ahead(value, [cache_keys, cache_values])
        return token

    jobs = [copy_query] + [functools.partial(copy_out, part) for part in range(4)]
    jobs = jobs + [copy_caches]

    def exchanged(value, bit):
        arrived = swapped(value, DEV, bit)
        return arrived, jobs.pop(0)(value) if jobs else jnp.zeros((8, LANES), F32)

    bit = 1
    while bit < n_dev:
        arrived, token = exchanged(sums, bit)
        bit *= 2
        if bit < n_dev:
            sums = joined(sums, arrived, token, True)
    query, fresh = queries(sums, arrived, token, q_gain, copied["query"])

    held, codes = query, [0]
    bit = n_dev // 2
    while bit:
        arrived, token = exchanged(held, bit)
        codes = codes + [code ^ bit for code in codes]
        bit //= 2
        if bit:
            held = joined(held, arrived, token, False)
    parts = attend(codes, place, lengths, token, [held, arrived], *copied["caches"])
    parts = lax.all_to_all(parts, DEV, 0, 0)
    head_sum = project(parts, query, fresh, copied["out"], w_out)
    if cols != head_sum.shape[2]:
        head_sum = head_sum.transpose(1, 0, 2).reshape(rows, n_dev, cols).transpose(1, 0, 2)
    head_sum = lax.all_to_all(head_sum.astype(BF16), DEV, 0, 0)
    residual = hidden_f + jnp.sum(head_sum.astype(F32), axis=0)

    squares = jnp.sum(residual * residual, axis=1)
    packed = jnp.concatenate(
        [residual * post_gain[None, :], jnp.broadcast_to(squares[:, None], (rows, LANES))],
        axis=1,
    )
    packed = gathered(packed, DEV)
    factor = lax.rsqrt(jnp.sum(packed[:, :, cols], axis=0) / D + EPS)
    normed = (packed[:, :, :cols] * factor[None, :, None]).astype(BF16)
    normed = normed.transpose(1, 0, 2).reshape(rows, n_dev * cols)
    n_far = lax.axis_size(FAR)
    arrived = swapped(normed, FAR, 1)
    (gate_t, up_t), token = ahead(normed, [w_gate.T, w_up.T])
    mine = joined(normed, arrived, token, False)
    other = swapped(mine, CORE, 1)
    (down,), token = ahead(mine, [w_down])
    ffn_term = ffn([mine, other], token, gate_t, up_t, down)

    half = n_far * rows
    ffn_term = ffn_term[:half] + swapped(ffn_term[half:], CORE, 1)
    ffn_term = ffn_term.reshape(n_far, rows, n_dev, cols)
    far = lax.axis_index(FAR)
    ffn_term = jnp.stack([lax.dynamic_index_in_dim(ffn_term, far ^ f, 0, False) for f in range(n_far)])
    ffn_term = ffn_term.transpose(0, 2, 1, 3).reshape(n_far * n_dev, rows, cols)
    ffn_term = lax.all_to_all(ffn_term.astype(BF16), (FAR, DEV), 0, 0)
    ffn_out = jnp.sum(ffn_term.astype(F32), axis=0)
    return residual + ffn_out


def solution(mesh):
    sizes = mesh.devices.shape
    mesh = jax.sharding.Mesh(
        mesh.devices.reshape(sizes[0] // 2, 2, sizes[1]), (FAR, CORE, DEV)
    )
    placed = (
        P(POOL, DEV),
        P(DEV),
        P(DEV, None),
        P(),
        P(None, DEV),
        P(POOL, DEV, None),
        P(POOL, DEV, None),
        P(POOL),
        P(DEV, None),
        P(DEV),
        P(None, (*POOL, DEV)),
        P(None, (*POOL, DEV)),
        P((*POOL, DEV), None),
    )
    return jax.shard_map(
        local, mesh=mesh, in_specs=placed, out_specs=P(POOL, DEV), check_vma=False
    )
```

```python
import functools
import math

import jax
import jax.numpy as jnp
from jax import lax
from jax.experimental import pallas as pl
from jax.experimental.pallas import tpu as pltpu
from jax.sharding import PartitionSpec as P

D = 7168
H = 64
HD = 256
QR = 2048
LATENT = QR + 2 * HD
LANES = 128
STATS = 16

EPS = 1e-05
NEG = -1e30

FAR, CORE, DEV = "far", "core", "dev"
POOL = (FAR, CORE)
F32, BF16 = jnp.float32, jnp.bfloat16
MIB = 1 << 20
VMEM = pl.BlockSpec(memory_space=pltpu.VMEM)
HBM = pl.BlockSpec(memory_space=pltpu.MemorySpace.HBM)


def dot(left, right, left_dim=1, right_dim=0):
    return lax.dot_general(
        left,
        right,
        (((left_dim,), (right_dim,)), ((), ())),
        preferred_element_type=F32,
    )


def whole(shape):
    return pl.BlockSpec(shape, lambda *_: (0,) * len(shape))


def params(mib):
    return pltpu.CompilerParams(vmem_limit_bytes=mib * MIB)


def streamed(weight):
    return pltpu.with_memory_space_constraint(weight, pltpu.MemorySpace.HBM)


def cost(flops, moved):
    return pl.CostEstimate(flops=flops, bytes_accessed=moved, transcendentals=0)


def started(source, target, sems, pieces, axis):
    width = source.shape[axis] // pieces
    copies = []
    for piece in range(pieces):
        span = pl.ds(piece * width, width)
        at = (slice(None),) * axis + (span,)
        copy = pltpu.make_async_copy(source.at[at], target.at[at], sems.at[piece])
        copy.start()
        copies.append(copy)
    return copies


def latent_kernel(hidden_ref, gain_hbm, w_hbm, out_ref, w_ref, gain_ref, sems, gain_sem):
    gain_copy = pltpu.make_async_copy(gain_hbm, gain_ref, gain_sem)
    gain_copy.start()
    copies = started(w_hbm, w_ref, sems, sems.shape[0], 1)
    hidden = hidden_ref[...].astype(F32)
    squares = jnp.sum(hidden * hidden, axis=1, keepdims=True)
    out_ref[:, LATENT:] = jnp.broadcast_to(squares, (hidden.shape[0], LANES))
    gain_copy.wait()
    scaled = (hidden * gain_ref[...][None, :]).astype(BF16)
    width = LATENT // len(copies)
    for step, copy in enumerate(copies):
        columns = slice(step * width, (step + 1) * width)
        copy.wait()
        out_ref[:, columns] = dot(scaled, w_ref[:, columns])


def latent_part(hidden, gain, w):
    rows, depth = hidden.shape
    return pl.pallas_call(
        latent_kernel,
        in_specs=[VMEM, HBM, HBM],
        out_specs=VMEM,
        out_shape=jax.ShapeDtypeStruct((rows, LATENT + LANES), F32),
        scratch_shapes=[
            pltpu.VMEM(w.shape, BF16),
            pltpu.VMEM(gain.shape, F32),
            pltpu.SemaphoreType.DMA((5,)),
            pltpu.SemaphoreType.DMA,
        ],
        compiler_params=params(8),
        cost_estimate=cost(2 * rows * depth * LATENT, 2 * depth * LATENT),
    )(hidden, streamed(gain), streamed(w))


def ahead_kernel(count, *refs):
    sources, targets = refs[1 : 1 + count], refs[1 + count : 1 + 2 * count]
    token_ref, sems = refs[-2:]
    copies = []
    for index, (source, target) in enumerate(zip(sources, targets)):
        copies.append(pltpu.make_async_copy(source, target, sems.at[index]))
        copies[-1].start()
    token_ref[...] = jnp.zeros_like(token_ref)
    for copy in copies:
        copy.wait()


def ahead(beside, weights):
    count = len(weights)
    shapes = [w.shape for w in weights]
    *copied, token = pl.pallas_call(
        functools.partial(ahead_kernel, count),
        in_specs=[pl.BlockSpec(memory_space=pl.ANY)] + [HBM] * count,
        out_specs=[VMEM] * (count + 1),
        out_shape=[pltpu.VMEM(shape, BF16) for shape in shapes]
        + [jax.ShapeDtypeStruct((8, LANES), F32)],
        scratch_shapes=[pltpu.SemaphoreType.DMA((count,))],
        compiler_params=params(1),
        cost_estimate=cost(0, sum(2 * math.prod(shape) for shape in shapes)),
    )(beside, *[streamed(w) for w in weights])
    return copied, token


def part_ahead(beside, weight, first, height, total, held):
    def kernel(*refs):
        source, (target, token_ref, sem) = refs[1], refs[-3:]
        rows = pl.ds(first, height)
        copy = pltpu.make_async_copy(source.at[rows], target.at[rows], sem)
        copy.start()
        token_ref[...] = jnp.zeros_like(token_ref)
        copy.wait()

    buffers = [] if held is None else [held]
    return pl.pallas_call(
        kernel,
        in_specs=[pl.BlockSpec(memory_space=pl.ANY), HBM] + [VMEM] * len(buffers),
        out_specs=[VMEM] * 2,
        out_shape=[
            pltpu.VMEM((total, weight.shape[1]), BF16),
            jax.ShapeDtypeStruct((8, LANES), F32),
        ],
        scratch_shapes=[pltpu.SemaphoreType.DMA],
        input_output_aliases={2: 0} if buffers else {},
        compiler_params=params(1),
        cost_estimate=cost(0, 2 * height * weight.shape[1]),
    )(beside, streamed(weight), *buffers)


def joined(left, right, token, add):
    def kernel(left_ref, right_ref, token_ref, out_ref):
        if add:
            out_ref[...] = left_ref[...] + right_ref[...]
        else:
            both = [left_ref[...].astype(F32), right_ref[...].astype(F32)]
            out_ref[...] = jnp.concatenate(both, axis=0).astype(out_ref.dtype)

    rows, cols = left.shape
    return pl.pallas_call(
        kernel,
        in_specs=[VMEM] * 3,
        out_specs=VMEM,
        out_shape=jax.ShapeDtypeStruct((rows if add else 2 * rows, cols), left.dtype),
        compiler_params=params(2),
        cost_estimate=cost(0, 3 * rows * cols * left.dtype.itemsize),
    )(left, right, token)


def summed(value, arrived, token):
    def kernel(value_ref, arrived_ref, token_ref, out_ref, sent_ref):
        total = value_ref[...] + arrived_ref[...].astype(F32)
        out_ref[...] = total
        sent_ref[...] = total.astype(BF16)

    shape = value.shape
    return pl.pallas_call(
        kernel,
        in_specs=[VMEM] * 3,
        out_specs=[VMEM] * 2,
        out_shape=[jax.ShapeDtypeStruct(shape, F32), jax.ShapeDtypeStruct(shape, BF16)],
        compiler_params=params(2),
        cost_estimate=cost(0, 12 * math.prod(shape)),
    )(value, arrived, token)


def normed_rows(place, value, arrived, token, hidden):
    rows, n_dev = value.shape[0], hidden.shape[0]
    cols = D // n_dev

    def kernel(place_ref, value_ref, arrived_ref, token_ref, hidden_ref, own_ref, normed_ref, wide_ref):
        squares = jnp.zeros((rows, 1), F32)
        for d in range(n_dev):
            span = slice(d * cols, (d + 1) * cols)
            attn = value_ref[:, span] + arrived_ref[:, span].astype(F32)
            residual = hidden_ref[d, :rows, :cols] + attn
            wide_ref[d] = residual
            squares += jnp.sum(residual * residual, axis=1, keepdims=True)
        factor = lax.rsqrt(squares / D + EPS)
        for d in range(n_dev):
            span = slice(d * cols, (d + 1) * cols)
            scaled = wide_ref[d] * factor * hidden_ref[d, rows : rows + 1, :cols]
            normed_ref[:, span] = scaled.astype(BF16)
        own_ref[...] = wide_ref[place_ref[0]]

    return pl.pallas_call(
        kernel,
        in_specs=[pl.BlockSpec(memory_space=pltpu.SMEM)] + [VMEM] * 4,
        out_specs=[VMEM] * 2,
        out_shape=[jax.ShapeDtypeStruct((rows, cols), F32), jax.ShapeDtypeStruct((rows, D), BF16)],
        scratch_shapes=[pltpu.VMEM((n_dev, rows, cols), F32)],
        compiler_params=params(3),
        cost_estimate=cost(0, 16 * rows * D),
    )(place, value, arrived, token, hidden)


def parts_of(value):
    high = value.astype(BF16).astype(F32)
    middle = (value - high).astype(BF16).astype(F32)
    return high, middle, value - high - middle


def query_kernel(
    left_ref, right_ref, token_ref, gain_ref, hidden_ref, next_ref, w_ref, query_ref, fresh_ref, wide_ref
):
    sums_ref = left_ref[...] + right_ref[...]
    rows, cols = hidden_ref.shape
    out = w_ref.shape[1]
    width = min(512, out)
    heads = out // HD
    factor = lax.rsqrt(sums_ref[:, LATENT : LATENT + 1] / D + EPS)
    query_latent = sums_ref[:, :QR] * factor
    mean = jnp.sum(query_latent * query_latent, axis=1, keepdims=True) / QR
    normed = (query_latent * lax.rsqrt(mean + EPS) * gain_ref[...]).astype(BF16)
    fresh = sums_ref[:, QR:LATENT] * factor
    fresh_ref[...] = fresh.astype(BF16).astype(F32)
    at = rows * heads
    hidden = hidden_ref[...].astype(F32)
    wide_ref[at:, :] = jnp.zeros((wide_ref.shape[0] - at, HD), F32)
    gains = parts_of(next_ref[...][None, :])
    for first in range(0, cols, HD):
        part = min(HD, cols - first)
        wide_ref[at : at + rows, :part] = hidden[:, first : first + part]
        at += rows
    for first in range(0, cols, HD):
        part = min(HD, cols - first)
        for gain in gains:
            wide_ref[at : at + 1, :part] = gain[:, first : first + part]
            at += 1
    for step in range(out // width):
        query = dot(normed, w_ref[:, step * width : (step + 1) * width])
        for part in range(width // HD):
            head = step * (width // HD) + part
            for row in range(rows):
                wide_ref[row * heads + head : row * heads + head + 1, :] = query[
                    row : row + 1, part * HD : (part + 1) * HD
                ]
    query_ref[...] = wide_ref[...].astype(BF16)


def queries(left, right, token, gain, hidden, next_gain, w):
    rows, cols = hidden.shape
    out = w.shape[1]
    heads = out // HD
    height = -(-(rows * heads + (rows + 3) * -(-cols // HD)) // 16) * 16
    return pl.pallas_call(
        query_kernel,
        in_specs=[VMEM] * 7,
        out_specs=[VMEM] * 2,
        out_shape=[
            jax.ShapeDtypeStruct((height, HD), BF16),
            jax.ShapeDtypeStruct((rows, 2 * HD), F32),
        ],
        scratch_shapes=[pltpu.VMEM((height, HD), F32)],
        compiler_params=params(2),
        cost_estimate=cost(2 * rows * QR * out, 2 * QR * out),
    )(left, right, token, gain.reshape(1, QR), hidden, next_gain, w)


def put_stats(ref, index, at, stats):
    heads = stats.shape[0]
    high, middle, low = parts_of(stats)
    ref[index, at:, :] = jnp.zeros((STATS, HD), F32)
    ref[index, at : at + heads, :LANES] = high
    ref[index, at : at + heads, LANES:] = middle
    ref[index, at + 8 : at + 8 + heads, :LANES] = low


def sent_stats(ref, index, at, heads):
    high = ref[index, at : at + heads, :LANES]
    middle = ref[index, at : at + heads, LANES:]
    return high + middle + ref[index, at + 8 : at + 8 + heads, :LANES]


def attend_kernel(codes, place_ref, lengths_ref, token_ref, *refs):
    n_dev = len(codes)
    pieces, refs = refs[:-8], refs[-8:]
    keys_ref, values_ref, own_ref, sent_ref, hidden_ref, wide_ref, parts_ref, weights_ref = refs
    rows, local_pos = keys_ref.shape[:2]
    heads = H // n_dev
    height = wide_ref.shape[0] // n_dev
    me = place_ref[0]
    at = 0
    for piece in pieces:
        size = piece.shape[0]
        wide_ref[at : at + size, :] = piece[...].astype(F32)
        at += size
    blocks = hidden_ref.shape[2] // HD
    for g in range(n_dev):
        first = g * height + rows * heads
        for block in range(blocks):
            span = slice(block * HD, (block + 1) * HD)
            at = first + block * rows
            hidden_ref[me ^ codes[g], :rows, span] = wide_ref[at : at + rows, :]
            at = first + blocks * rows + 3 * block
            gain = wide_ref[at : at + 1, :] + wide_ref[at + 1 : at + 2, :]
            hidden_ref[me ^ codes[g], rows : rows + 1, span] = gain + wide_ref[at + 2 : at + 3, :]
    lane = lax.broadcasted_iota(jnp.int32, (H, LANES), 1)
    columns = lax.broadcasted_iota(jnp.int32, (H, local_pos), 1) + me * local_pos
    stats = jnp.zeros((H, LANES), F32)
    for row in range(rows):
        query = jnp.concatenate(
            [
                wide_ref[g * height + row * heads : g * height + (row + 1) * heads, :]
                for g in range(n_dev)
            ],
            axis=0,
        ).astype(BF16)
        scores = dot(query, keys_ref[row], 1, 1) * (1.0 / math.sqrt(HD))
        valid = columns < lengths_ref[row]
        masked = jnp.where(valid, scores, NEG)
        top = jnp.max(masked, axis=1, keepdims=True)
        weights = jnp.where(valid, jnp.exp(masked - top), 0.0)
        mass = jnp.sum(weights, axis=1, keepdims=True)
        weights_ref[row] = weights.astype(BF16)
        stats = jnp.where(lane == row, top, stats)
        stats = jnp.where(lane == rows + row, mass, stats)
    half = n_dev // 2
    for row in range(rows):
        weighted = dot(weights_ref[row], values_ref[row])
        for g in range(n_dev):
            target = own_ref if g < half else parts_ref
            target[g % half, row * heads : (row + 1) * heads, :] = weighted[
                g * heads : (g + 1) * heads, :
            ]
    at = rows * heads
    for g in range(half):
        own_ref[g, at:, :] = jnp.zeros((STATS, HD), F32)
        own_ref[g, at : at + heads, :LANES] = stats[g * heads : (g + 1) * heads]
        put_stats(parts_ref, g, at, stats[(half + g) * heads : (half + g + 1) * heads])
    sent_ref[...] = parts_ref[...].astype(BF16)


def attend(codes, place, lengths, token, pieces, keys, values):
    rows, local_pos = keys.shape[:2]
    n_dev = len(codes)
    half = (n_dev // 2, rows * H // n_dev + STATS, HD)
    hidden_width = -(-D // n_dev // HD) * HD
    smem = pl.BlockSpec(memory_space=pltpu.SMEM)
    return pl.pallas_call(
        functools.partial(attend_kernel, codes),
        in_specs=[smem, smem] + [VMEM] * (3 + len(pieces)),
        out_specs=[VMEM] * 3,
        out_shape=[
            jax.ShapeDtypeStruct(half, F32),
            jax.ShapeDtypeStruct(half, BF16),
            jax.ShapeDtypeStruct((n_dev, rows + 8, hidden_width), F32),
        ],
        scratch_shapes=[
            pltpu.VMEM((sum(piece.shape[0] for piece in pieces), HD), F32),
            pltpu.VMEM(half, F32),
            pltpu.VMEM((rows, H, local_pos), BF16),
        ],
        compiler_params=params(5),
        cost_estimate=cost(4 * rows * H * local_pos * HD, 4 * rows * local_pos * HD),
    )(place, lengths, token, *pieces, keys, values)


def merge_kernel(rows, own_ref, arrived_ref, token_ref, out_ref, sent_ref, wide_ref, parts_ref):
    count, height, _ = own_ref.shape
    at = height - STATS
    heads = at // rows
    wide_ref[...] = arrived_ref[...].astype(F32)
    lane = lax.broadcasted_iota(jnp.int32, (heads, LANES), 1)
    half = count // 2
    for block in range(count):
        target = out_ref if block < half else parts_ref
        here = own_ref[block, at : at + heads, :LANES]
        there = sent_stats(wide_ref, block, at, heads)
        stats = jnp.zeros((heads, LANES), F32)
        for row in range(rows):
            span = slice(row * heads, (row + 1) * heads)
            top = jnp.maximum(here[:, row : row + 1], there[:, row : row + 1])
            left = jnp.exp(here[:, row : row + 1] - top)
            right = jnp.exp(there[:, row : row + 1] - top)
            mass = left * here[:, rows + row : rows + row + 1]
            mass = mass + right * there[:, rows + row : rows + row + 1]
            total = left * own_ref[block, span, :] + right * wide_ref[block, span, :]
            target[block % half, span, :] = total
            stats = jnp.where(lane == row, top, stats)
            stats = jnp.where(lane == rows + row, mass, stats)
        if block < half:
            target[block, at:, :] = jnp.zeros((STATS, HD), F32)
            target[block, at : at + heads, :LANES] = stats
        else:
            put_stats(target, block - half, at, stats)
    sent_ref[...] = parts_ref[...].astype(BF16)


def merge(rows, own, arrived, token):
    half = (own.shape[0] // 2, *own.shape[1:])
    return pl.pallas_call(
        functools.partial(merge_kernel, rows),
        in_specs=[VMEM] * 3,
        out_specs=[VMEM] * 2,
        out_shape=[jax.ShapeDtypeStruct(half, F32), jax.ShapeDtypeStruct(half, BF16)],
        scratch_shapes=[pltpu.VMEM(own.shape, F32), pltpu.VMEM(half, F32)],
        compiler_params=params(6),
        cost_estimate=cost(0, 12 * math.prod(own.shape)),
    )(own, arrived, token)


def project_kernel(
    own_ref, arrived_ref, token_ref, query_ref, fresh_ref, held_ref, w_hbm, out_ref, sent_ref, *scratch
):
    attended_ref, wide_ref, w_ref, sems = scratch
    held, steps = held_ref.shape[0], sems.shape[0]
    copies = started(w_hbm.at[held : held + w_ref.shape[0]], w_ref, sems, steps, 1)
    rows = fresh_ref.shape[0]
    at = own_ref.shape[1] - STATS
    heads = at // rows
    query = query_ref[...].astype(F32)
    wide_ref[...] = arrived_ref[...].astype(F32)
    parts = [
        (own_ref, own_ref[0, at : at + heads, :LANES]),
        (wide_ref, sent_stats(wide_ref, 0, at, heads)),
    ]
    for row in range(rows):
        span = slice(row * heads, (row + 1) * heads)
        key = fresh_ref[row : row + 1, :HD]
        value = fresh_ref[row : row + 1, HD:]
        score = jnp.sum(query[span] * key, axis=1, keepdims=True) * (1.0 / math.sqrt(HD))
        highest = score
        for _, stats in parts:
            highest = jnp.maximum(highest, stats[:, row : row + 1])
        weight = jnp.exp(score - highest)
        mass = weight
        total = weight.astype(BF16).astype(F32) * value
        for ref, stats in parts:
            factor = jnp.exp(stats[:, row : row + 1] - highest)
            mass = mass + factor * stats[:, rows + row : rows + row + 1]
            total = total + factor * ref[0, span, :]
        attended = total / mass
        for head in range(heads):
            attended_ref[row : row + 1, head * HD : (head + 1) * HD] = attended[
                head : head + 1, :
            ]
    width = D // steps
    attended = attended_ref[...].astype(BF16)
    for step, copy in enumerate(copies):
        columns = slice(step * width, (step + 1) * width)
        total = dot(attended[:, :held], held_ref[:, columns])
        copy.wait()
        total = total + dot(attended[:, held:], w_ref[:, columns])
        out_ref[:, columns] = total
        sent_ref[:, columns] = total.astype(BF16)


def project(own, arrived, token, query, fresh, held, w):
    rows = fresh.shape[0]
    depth = w.shape[0]
    return pl.pallas_call(
        project_kernel,
        in_specs=[VMEM] * 6 + [HBM],
        out_specs=[VMEM] * 2,
        out_shape=[jax.ShapeDtypeStruct((rows, D), F32), jax.ShapeDtypeStruct((rows, D), BF16)],
        scratch_shapes=[
            pltpu.VMEM((rows, depth), F32),
            pltpu.VMEM(own.shape, F32),
            pltpu.VMEM((depth - held.shape[0], D), BF16),
            pltpu.SemaphoreType.DMA((8,)),
        ],
        compiler_params=params(16),
        cost_estimate=cost(2 * rows * depth * D, 2 * depth * D),
    )(own, arrived, token, query, fresh, held, streamed(w))


def ffn_kernel(*refs):
    pieces, refs = refs[:-7], refs[-7:]
    token_ref, gate_ref, up_ref, down_ref, own_ref, other_ref, act_ref = refs
    half = own_ref.shape[0]
    rows = jnp.concatenate([piece[...] for piece in pieces], axis=0)
    units = gate_ref.shape[0]
    block = 144
    for step in range(units // block):
        span = slice(step * block, (step + 1) * block)
        gate = dot(gate_ref[span, :], rows, 1, 1)
        up = dot(up_ref[span, :], rows, 1, 1)
        act_ref[span, :] = gate / (1.0 + jnp.exp(-gate)) * up
    activated = act_ref[...].astype(BF16)
    width = down_ref.shape[1] // 8

    @pl.loop(0, 8)
    def _(step):
        columns = pl.ds(pl.multiple_of(step * width, width), width)
        term = dot(activated, down_ref[:, columns], 0, 0)
        own_ref[:, columns] = term[:half]
        other_ref[:, columns] = term[half:]


def ffn(pieces, token, gate_t, up_t, down):
    rows = sum(piece.shape[0] for piece in pieces)
    units, depth = gate_t.shape
    return pl.pallas_call(
        ffn_kernel,
        in_specs=[VMEM] * (len(pieces) + 4),
        out_specs=[VMEM] * 2,
        out_shape=[jax.ShapeDtypeStruct((rows // 2, depth), F32)] * 2,
        scratch_shapes=[pltpu.VMEM((units, rows), F32)],
        compiler_params=params(6),
        cost_estimate=cost(6 * rows * units * depth, 6 * units * depth),
    )(*pieces, token, gate_t, up_t, down)


def combined(far, own, arrived, n_far, n_dev):
    rows, cols = own.shape[0] // n_far, own.shape[1] // n_dev

    def kernel(far_ref, own_ref, arrived_ref, out_ref, wide_ref):
        for f in range(n_far):
            target = (far_ref[0] ^ f) * n_dev
            for d in range(n_dev):
                at = (slice(f * rows, (f + 1) * rows), slice(d * cols, (d + 1) * cols))
                wide_ref[target + d] = own_ref[at] + arrived_ref[at]
        out_ref[...] = wide_ref[...].astype(BF16)

    shape = (n_far * n_dev, rows, cols)
    return pl.pallas_call(
        kernel,
        in_specs=[pl.BlockSpec(memory_space=pltpu.SMEM)] + [VMEM] * 2,
        out_specs=VMEM,
        out_shape=jax.ShapeDtypeStruct(shape, BF16),
        scratch_shapes=[pltpu.VMEM(shape, F32)],
        compiler_params=params(4),
        cost_estimate=cost(0, 10 * math.prod(shape)),
    )(far, own, arrived)


def swapped(value, axis, bit):
    size = lax.axis_size(axis)
    return lax.ppermute(value, axis, [(i, i ^ bit) for i in range(size)])


def gathered(value, axis):
    size = lax.axis_size(axis)
    return lax.all_to_all(jnp.broadcast_to(value[None], (size, *value.shape)), axis, 0, 0)


def local(
    hidden_in,
    in_gain,
    w_latent,
    q_gain,
    w_query,
    cache_keys,
    cache_values,
    lengths,
    w_out,
    post_gain,
    w_gate,
    w_up,
    w_down,
):
    n_dev = lax.axis_size(DEV)
    place = lax.axis_index(DEV).astype(jnp.int32).reshape(1)
    rows, cols = hidden_in.shape

    sums = latent_part(hidden_in, in_gain, w_latent)
    copied = {}

    def copy_query(value):
        (copied["query"],), token = ahead(value, [w_query])
        return token


    def copy_out(first, height, total, value):
        held = copied.get("out")
        copied["out"], token = part_ahead(value, w_out, first, height, total, held)
        return token

    def copy_caches(value):
        copied["caches"], token = ahead(value, [cache_keys, cache_values])
        return token

    def copy_ffn(name, weight, value):
        (copied[name],), token = ahead(value, [weight])
        return token

    steps = n_dev.bit_length() - 1
    jobs = [copy_query] + [None] * (2 * steps - 2) + [copy_caches]
    block = w_out.shape[0] // 16
    heights = [4 * block, 3 * block, 3 * block] + [0] * (steps - 3)
    for step, height in enumerate(heights):
        first = sum(heights[:step])
        jobs.append(functools.partial(copy_out, first, height, sum(heights)) if height else None)
    for name, weight in (("gate", w_gate.T), ("up", w_up.T), ("down", w_down)):
        jobs.append(functools.partial(copy_ffn, name, weight))
    jobs += [None] * (steps - 3)

    def exchanged(value, bit):
        arrived = swapped(value, DEV, bit)
        job = jobs.pop(0)
        copied["token"] = job(value) if job else copied["token"]
        return arrived, copied["token"]

    bit = 1
    while bit < n_dev:
        arrived, token = exchanged(sums, bit)
        bit *= 2
        if bit < n_dev:
            sums = joined(sums, arrived, token, True)
    query, fresh = queries(
        sums, arrived, token, q_gain, hidden_in, post_gain, copied["query"]
    )

    held, codes = query, [0]
    bit = n_dev // 2
    while bit:
        arrived, token = exchanged(held, bit)
        codes = codes + [code ^ bit for code in codes]
        bit //= 2
        if bit:
            held = joined(held, arrived, token, False)
    own, sent, hidden = attend(
        codes, place, lengths, token, [held, arrived], *copied["caches"]
    )

    bit = 1
    while bit < n_dev:
        arrived, token = exchanged(sent, bit)
        bit *= 2
        if bit < n_dev:
            own, sent = merge(rows, own, arrived, token)
    attn, sent = project(own, arrived, token, query, fresh, copied["out"], w_out)

    bit = 1
    while bit < n_dev:
        arrived, token = exchanged(sent, bit)
        bit *= 2
        if bit < n_dev:
            attn, sent = summed(attn, arrived, token)
    residual, normed = normed_rows(place, attn, arrived, token, hidden)
    n_far = lax.axis_size(FAR)
    arrived = swapped(normed, FAR, 1)
    mine = joined(normed, arrived, token, False)
    other = swapped(mine, CORE, 1)
    own, other = ffn([mine, other], token, copied["gate"], copied["up"], copied["down"])

    far = lax.axis_index(FAR).astype(jnp.int32).reshape(1)
    ffn_term = combined(far, own, swapped(other, CORE, 1), n_far, n_dev)
    ffn_term = lax.all_to_all(ffn_term, (FAR, DEV), 0, 0)
    ffn_out = jnp.sum(ffn_term.astype(F32), axis=0)
    return residual + ffn_out


def solution(mesh):
    sizes = mesh.devices.shape
    mesh = jax.sharding.Mesh(
        mesh.devices.reshape(sizes[0] // 2, 2, sizes[1]), (FAR, CORE, DEV)
    )
    placed = (
        P(POOL, DEV),
        P(DEV),
        P(DEV, None),
        P(),
        P(None, DEV),
        P(POOL, DEV, None),
        P(POOL, DEV, None),
        P(POOL),
        P(DEV, None),
        P(DEV),
        P(None, (*POOL, DEV)),
        P(None, (*POOL, DEV)),
        P((*POOL, DEV), None),
    )
    return jax.shard_map(
        local, mesh=mesh, in_specs=placed, out_specs=P(POOL, DEV), check_vma=False
    )
```

```python
import functools
import math

import jax
import jax.numpy as jnp
from jax import lax
from jax.experimental import pallas as pl
from jax.experimental.pallas import tpu as pltpu
from jax.sharding import PartitionSpec as P

D = 7168
H = 64
HD = 256
QR = 2048
LATENT = QR + 2 * HD
LANES = 128
STATS = 16

EPS = 1e-05
NEG = -1e30

FAR, CORE, DEV = "far", "core", "dev"
POOL = (FAR, CORE)
F32, BF16 = jnp.float32, jnp.bfloat16
MIB = 1 << 20
VMEM = pl.BlockSpec(memory_space=pltpu.VMEM)
HBM = pl.BlockSpec(memory_space=pltpu.MemorySpace.HBM)


def dot(left, right, left_dim=1, right_dim=0):
    return lax.dot_general(
        left,
        right,
        (((left_dim,), (right_dim,)), ((), ())),
        preferred_element_type=F32,
    )


def whole(shape):
    return pl.BlockSpec(shape, lambda *_: (0,) * len(shape))


def params(mib):
    return pltpu.CompilerParams(vmem_limit_bytes=mib * MIB)


def streamed(weight):
    return pltpu.with_memory_space_constraint(weight, pltpu.MemorySpace.HBM)


def cost(flops, moved):
    return pl.CostEstimate(flops=flops, bytes_accessed=moved, transcendentals=0)


def started(source, target, sems, pieces, axis):
    width = source.shape[axis] // pieces
    copies = []
    for piece in range(pieces):
        span = pl.ds(piece * width, width)
        at = (slice(None),) * axis + (span,)
        copy = pltpu.make_async_copy(source.at[at], target.at[at], sems.at[piece])
        copy.start()
        copies.append(copy)
    return copies


def latent_kernel(hidden_ref, gain_hbm, w_hbm, out_ref, w_ref, gain_ref, sems, gain_sem):
    gain_copy = pltpu.make_async_copy(gain_hbm, gain_ref, gain_sem)
    gain_copy.start()
    copies = started(w_hbm, w_ref, sems, sems.shape[0], 1)
    hidden = hidden_ref[...].astype(F32)
    squares = jnp.sum(hidden * hidden, axis=1, keepdims=True)
    out_ref[:, LATENT:] = jnp.broadcast_to(squares, (hidden.shape[0], LANES))
    gain_copy.wait()
    scaled = (hidden * gain_ref[...][None, :]).astype(BF16)
    width = LATENT // len(copies)
    for step, copy in enumerate(copies):
        columns = slice(step * width, (step + 1) * width)
        copy.wait()
        out_ref[:, columns] = dot(scaled, w_ref[:, columns])


def latent_part(hidden, gain, w):
    rows, depth = hidden.shape
    return pl.pallas_call(
        latent_kernel,
        in_specs=[VMEM, HBM, HBM],
        out_specs=VMEM,
        out_shape=jax.ShapeDtypeStruct((rows, LATENT + LANES), F32),
        scratch_shapes=[
            pltpu.VMEM(w.shape, BF16),
            pltpu.VMEM(gain.shape, F32),
            pltpu.SemaphoreType.DMA((5,)),
            pltpu.SemaphoreType.DMA,
        ],
        compiler_params=params(8),
        cost_estimate=cost(2 * rows * depth * LATENT, 2 * depth * LATENT),
    )(hidden, streamed(gain), streamed(w))


def ahead_kernel(count, *refs):
    sources, targets = refs[1 : 1 + count], refs[1 + count : 1 + 2 * count]
    token_ref, sems = refs[-2:]
    copies = []
    for index, (source, target) in enumerate(zip(sources, targets)):
        view = source if source.shape == target.shape else source.at[:, : target.shape[1]]
        copies.append(pltpu.make_async_copy(view, target, sems.at[index]))
        copies[-1].start()
    token_ref[...] = jnp.zeros_like(token_ref)
    for copy in copies:
        copy.wait()


def ahead(beside, weights, columns=None):
    count = len(weights)
    shapes = [w.shape if columns is None else (w.shape[0], columns) for w in weights]
    *copied, token = pl.pallas_call(
        functools.partial(ahead_kernel, count),
        in_specs=[pl.BlockSpec(memory_space=pl.ANY)] + [HBM] * count,
        out_specs=[VMEM] * (count + 1),
        out_shape=[pltpu.VMEM(shape, BF16) for shape in shapes]
        + [jax.ShapeDtypeStruct((8, LANES), F32)],
        scratch_shapes=[pltpu.SemaphoreType.DMA((count,))],
        compiler_params=params(1),
        cost_estimate=cost(0, sum(2 * math.prod(shape) for shape in shapes)),
    )(beside, *[streamed(w) for w in weights])
    return copied, token


def joined(left, right, token, add):
    def kernel(left_ref, right_ref, token_ref, out_ref):
        if add:
            out_ref[...] = left_ref[...] + right_ref[...]
        else:
            both = [left_ref[...].astype(F32), right_ref[...].astype(F32)]
            out_ref[...] = jnp.concatenate(both, axis=0).astype(out_ref.dtype)

    rows, cols = left.shape
    return pl.pallas_call(
        kernel,
        in_specs=[VMEM] * 3,
        out_specs=VMEM,
        out_shape=jax.ShapeDtypeStruct((rows if add else 2 * rows, cols), left.dtype),
        compiler_params=params(2),
        cost_estimate=cost(0, 3 * rows * cols * left.dtype.itemsize),
    )(left, right, token)


def summed(value, arrived, token):
    def kernel(value_ref, arrived_ref, token_ref, out_ref, sent_ref):
        total = value_ref[...] + arrived_ref[...].astype(F32)
        out_ref[...] = total
        sent_ref[...] = total.astype(BF16)

    shape = value.shape
    return pl.pallas_call(
        kernel,
        in_specs=[VMEM] * 3,
        out_specs=[VMEM] * 2,
        out_shape=[jax.ShapeDtypeStruct(shape, F32), jax.ShapeDtypeStruct(shape, BF16)],
        compiler_params=params(2),
        cost_estimate=cost(0, 12 * math.prod(shape)),
    )(value, arrived, token)


def normed_rows(place, value, arrived, token, hidden):
    rows, n_dev = value.shape[0], hidden.shape[0]
    cols = D // n_dev

    def kernel(place_ref, value_ref, arrived_ref, token_ref, hidden_ref, own_ref, normed_ref, wide_ref):
        squares = jnp.zeros((rows, 1), F32)
        for d in range(n_dev):
            span = slice(d * cols, (d + 1) * cols)
            attn = value_ref[:, span] + arrived_ref[:, span].astype(F32)
            residual = hidden_ref[d, :rows, :cols] + attn
            wide_ref[d] = residual
            squares += jnp.sum(residual * residual, axis=1, keepdims=True)
        factor = lax.rsqrt(squares / D + EPS)
        for d in range(n_dev):
            span = slice(d * cols, (d + 1) * cols)
            scaled = wide_ref[d] * factor * hidden_ref[d, rows : rows + 1, :cols]
            normed_ref[:, span] = scaled.astype(BF16)
        own_ref[...] = wide_ref[place_ref[0]]

    return pl.pallas_call(
        kernel,
        in_specs=[pl.BlockSpec(memory_space=pltpu.SMEM)] + [VMEM] * 4,
        out_specs=[VMEM] * 2,
        out_shape=[jax.ShapeDtypeStruct((rows, cols), F32), jax.ShapeDtypeStruct((rows, D), BF16)],
        scratch_shapes=[pltpu.VMEM((n_dev, rows, cols), F32)],
        compiler_params=params(3),
        cost_estimate=cost(0, 16 * rows * D),
    )(place, value, arrived, token, hidden)


def parts_of(value):
    high = value.astype(BF16).astype(F32)
    middle = (value - high).astype(BF16).astype(F32)
    return high, middle, value - high - middle


def query_kernel(
    left_ref, right_ref, token_ref, gain_ref, hidden_ref, next_ref, w_ref, query_ref, fresh_ref, wide_ref
):
    sums_ref = left_ref[...] + right_ref[...]
    rows, cols = hidden_ref.shape
    out = w_ref.shape[1]
    width = min(512, out)
    heads = out // HD
    factor = lax.rsqrt(sums_ref[:, LATENT : LATENT + 1] / D + EPS)
    query_latent = sums_ref[:, :QR] * factor
    mean = jnp.sum(query_latent * query_latent, axis=1, keepdims=True) / QR
    normed = (query_latent * lax.rsqrt(mean + EPS) * gain_ref[...]).astype(BF16)
    fresh = sums_ref[:, QR:LATENT] * factor
    fresh_ref[...] = fresh.astype(BF16).astype(F32)
    at = rows * heads
    hidden = hidden_ref[...].astype(F32)
    wide_ref[at:, :] = jnp.zeros((wide_ref.shape[0] - at, HD), F32)
    gains = parts_of(next_ref[...][None, :])
    for first in range(0, cols, HD):
        part = min(HD, cols - first)
        wide_ref[at : at + rows, :part] = hidden[:, first : first + part]
        at += rows
    for first in range(0, cols, HD):
        part = min(HD, cols - first)
        for gain in gains:
            wide_ref[at : at + 1, :part] = gain[:, first : first + part]
            at += 1
    for step in range(out // width):
        query = dot(normed, w_ref[:, step * width : (step + 1) * width])
        for part in range(width // HD):
            head = step * (width // HD) + part
            for row in range(rows):
                wide_ref[row * heads + head : row * heads + head + 1, :] = query[
                    row : row + 1, part * HD : (part + 1) * HD
                ]
    query_ref[...] = wide_ref[...].astype(BF16)


def queries(left, right, token, gain, hidden, next_gain, w):
    rows, cols = hidden.shape
    out = w.shape[1]
    heads = out // HD
    height = -(-(rows * heads + (rows + 3) * -(-cols // HD)) // 16) * 16
    return pl.pallas_call(
        query_kernel,
        in_specs=[VMEM] * 7,
        out_specs=[VMEM] * 2,
        out_shape=[
            jax.ShapeDtypeStruct((height, HD), BF16),
            jax.ShapeDtypeStruct((rows, 2 * HD), F32),
        ],
        scratch_shapes=[pltpu.VMEM((height, HD), F32)],
        compiler_params=params(2),
        cost_estimate=cost(2 * rows * QR * out, 2 * QR * out),
    )(left, right, token, gain.reshape(1, QR), hidden, next_gain, w)


def attend_kernel(codes, place_ref, lengths_ref, token_ref, *refs):
    n_dev = len(codes)
    pieces, refs = refs[:-7], refs[-7:]
    keys_ref, values_ref, out_ref, hidden_ref, wide_ref, parts_ref, weights_ref = refs
    rows, local_pos = keys_ref.shape[:2]
    heads = H // n_dev
    height = wide_ref.shape[0] // n_dev
    me = place_ref[0]
    at = 0
    for piece in pieces:
        size = piece.shape[0]
        wide_ref[at : at + size, :] = piece[...].astype(F32)
        at += size
    blocks = hidden_ref.shape[2] // HD
    for g in range(n_dev):
        first = g * height + rows * heads
        for block in range(blocks):
            span = slice(block * HD, (block + 1) * HD)
            at = first + block * rows
            hidden_ref[me ^ codes[g], :rows, span] = wide_ref[at : at + rows, :]
            at = first + blocks * rows + 3 * block
            gain = wide_ref[at : at + 1, :] + wide_ref[at + 1 : at + 2, :]
            hidden_ref[me ^ codes[g], rows : rows + 1, span] = gain + wide_ref[at + 2 : at + 3, :]
    lane = lax.broadcasted_iota(jnp.int32, (H, LANES), 1)
    columns = lax.broadcasted_iota(jnp.int32, (H, local_pos), 1) + me * local_pos
    stats = jnp.zeros((H, LANES), F32)
    for row in range(rows):
        query = jnp.concatenate(
            [
                wide_ref[g * height + row * heads : g * height + (row + 1) * heads, :]
                for g in range(n_dev)
            ],
            axis=0,
        ).astype(BF16)
        scores = dot(query, keys_ref[row], 1, 1) * (1.0 / math.sqrt(HD))
        valid = columns < lengths_ref[row]
        masked = jnp.where(valid, scores, NEG)
        top = jnp.max(masked, axis=1, keepdims=True)
        weights = jnp.where(valid, jnp.exp(masked - top), 0.0)
        mass = jnp.sum(weights, axis=1, keepdims=True)
        weights_ref[row] = weights.astype(BF16)
        stats = jnp.where(lane == row, top, stats)
        stats = jnp.where(lane == rows + row, mass, stats)
    for row in range(rows):
        weighted = dot(weights_ref[row], values_ref[row])
        for g in range(n_dev):
            parts_ref[me ^ codes[g], row * heads : (row + 1) * heads, :] = weighted[
                g * heads : (g + 1) * heads, :
            ]
    high, middle, low = parts_of(stats)
    at = rows * heads
    parts_ref[:, at:, :] = jnp.zeros((n_dev, STATS, HD), F32)
    for g in range(n_dev):
        span = slice(g * heads, (g + 1) * heads)
        parts_ref[me ^ codes[g], at : at + heads, :LANES] = high[span]
        parts_ref[me ^ codes[g], at : at + heads, LANES:] = middle[span]
        parts_ref[me ^ codes[g], at + 8 : at + 8 + heads, :LANES] = low[span]
    out_ref[...] = parts_ref[...].astype(BF16)


def attend(codes, place, lengths, token, pieces, keys, values):
    rows, local_pos = keys.shape[:2]
    n_dev = len(codes)
    height = rows * H // n_dev + STATS
    hidden_width = -(-D // n_dev // HD) * HD
    smem = pl.BlockSpec(memory_space=pltpu.SMEM)
    return pl.pallas_call(
        functools.partial(attend_kernel, codes),
        in_specs=[smem, smem] + [VMEM] * (3 + len(pieces)),
        out_specs=[VMEM] * 2,
        out_shape=[
            jax.ShapeDtypeStruct((n_dev, height, HD), BF16),
            jax.ShapeDtypeStruct((n_dev, rows + 8, hidden_width), F32),
        ],
        scratch_shapes=[
            pltpu.VMEM((sum(piece.shape[0] for piece in pieces), HD), F32),
            pltpu.VMEM((n_dev, height, HD), F32),
            pltpu.VMEM((rows, H, local_pos), BF16),
        ],
        compiler_params=params(5),
        cost_estimate=cost(4 * rows * H * local_pos * HD, 4 * rows * local_pos * HD),
    )(place, lengths, token, *pieces, keys, values)


def project_kernel(
    sent_ref, query_ref, fresh_ref, held_ref, w_hbm, out_ref, half_ref, attended_ref, parts_ref, w_ref, sems
):
    n_dev = sent_ref.shape[0]
    held, width = held_ref.shape[1], D // 8
    copies = started(w_hbm.at[:, held:], w_ref, sems, sems.shape[0], 1)
    rows = fresh_ref.shape[0]
    heads = H // n_dev
    query = query_ref[...].astype(F32)
    parts_ref[...] = sent_ref[...].astype(F32)
    at = rows * heads
    stats = [
        parts_ref[d, at : at + heads, :LANES]
        + parts_ref[d, at : at + heads, LANES:]
        + parts_ref[d, at + 8 : at + 8 + heads, :LANES]
        for d in range(n_dev)
    ]
    for row in range(rows):
        span = slice(row * heads, (row + 1) * heads)
        key = fresh_ref[row : row + 1, :HD]
        value = fresh_ref[row : row + 1, HD:]
        score = jnp.sum(query[span] * key, axis=1, keepdims=True) * (1.0 / math.sqrt(HD))
        highest = score
        for d in range(n_dev):
            highest = jnp.maximum(highest, stats[d][:, row : row + 1])
        weight = jnp.exp(score - highest)
        mass = weight
        total = weight.astype(BF16).astype(F32) * value
        for d in range(n_dev):
            factor = jnp.exp(stats[d][:, row : row + 1] - highest)
            mass = mass + factor * stats[d][:, rows + row : rows + row + 1]
            total = total + factor * parts_ref[d, span, :]
        attended = total / mass
        for head in range(heads):
            attended_ref[row : row + 1, head * HD : (head + 1) * HD] = attended[
                head : head + 1, :
            ]

    attended = attended_ref[...].astype(BF16)
    for first in range(0, D, width):
        columns = slice(first, first + width)
        if first < held:
            total = dot(attended, held_ref[:, columns])
        else:
            copies[(first - held) // width].wait()
            total = dot(attended, w_ref[:, first - held : first - held + width])
        out_ref[:, columns] = total
        half_ref[:, columns] = total.astype(BF16)


def project(parts, query, fresh, held, w):
    rows = fresh.shape[0]
    depth = w.shape[0]
    width = D // 8
    return pl.pallas_call(
        project_kernel,
        in_specs=[VMEM] * 4 + [HBM],
        out_specs=[VMEM] * 2,
        out_shape=[jax.ShapeDtypeStruct((rows, D), F32), jax.ShapeDtypeStruct((rows, D), BF16)],
        scratch_shapes=[
            pltpu.VMEM((rows, depth), F32),
            pltpu.VMEM(parts.shape, F32),
            pltpu.VMEM((depth, D - held.shape[1]), BF16),
            pltpu.SemaphoreType.DMA(((D - held.shape[1]) // width,)),
        ],
        compiler_params=params(28),
        cost_estimate=cost(2 * rows * depth * D, 2 * depth * D),
    )(parts, query, fresh, held, streamed(w))


def ffn_kernel(*refs):
    pieces, refs = refs[:-7], refs[-7:]
    token_ref, gate_ref, up_ref, down_ref, own_ref, other_ref, act_ref = refs
    half = own_ref.shape[0]
    rows = jnp.concatenate([piece[...] for piece in pieces], axis=0)
    units = gate_ref.shape[0]
    block = 144
    for step in range(units // block):
        span = slice(step * block, (step + 1) * block)
        gate = dot(gate_ref[span, :], rows, 1, 1)
        up = dot(up_ref[span, :], rows, 1, 1)
        act_ref[span, :] = gate / (1.0 + jnp.exp(-gate)) * up
    activated = act_ref[...].astype(BF16)
    width = down_ref.shape[1] // 8

    @pl.loop(0, 8)
    def _(step):
        columns = pl.ds(pl.multiple_of(step * width, width), width)
        term = dot(activated, down_ref[:, columns], 0, 0)
        own_ref[:, columns] = term[:half]
        other_ref[:, columns] = term[half:]


def ffn(pieces, token, gate_t, up_t, down):
    rows = sum(piece.shape[0] for piece in pieces)
    units, depth = gate_t.shape
    return pl.pallas_call(
        ffn_kernel,
        in_specs=[VMEM] * (len(pieces) + 4),
        out_specs=[VMEM] * 2,
        out_shape=[jax.ShapeDtypeStruct((rows // 2, depth), F32)] * 2,
        scratch_shapes=[pltpu.VMEM((units, rows), F32)],
        compiler_params=params(6),
        cost_estimate=cost(6 * rows * units * depth, 6 * units * depth),
    )(*pieces, token, gate_t, up_t, down)


def combined(far, own, arrived, n_far, n_dev):
    rows, cols = own.shape[0] // n_far, own.shape[1] // n_dev

    def kernel(far_ref, own_ref, arrived_ref, out_ref, wide_ref):
        for f in range(n_far):
            target = (far_ref[0] ^ f) * n_dev
            for d in range(n_dev):
                at = (slice(f * rows, (f + 1) * rows), slice(d * cols, (d + 1) * cols))
                wide_ref[target + d] = own_ref[at] + arrived_ref[at]
        out_ref[...] = wide_ref[...].astype(BF16)

    shape = (n_far * n_dev, rows, cols)
    return pl.pallas_call(
        kernel,
        in_specs=[pl.BlockSpec(memory_space=pltpu.SMEM)] + [VMEM] * 2,
        out_specs=VMEM,
        out_shape=jax.ShapeDtypeStruct(shape, BF16),
        scratch_shapes=[pltpu.VMEM(shape, F32)],
        compiler_params=params(4),
        cost_estimate=cost(0, 10 * math.prod(shape)),
    )(far, own, arrived)


def swapped(value, axis, bit):
    size = lax.axis_size(axis)
    return lax.ppermute(value, axis, [(i, i ^ bit) for i in range(size)])


def gathered(value, axis):
    size = lax.axis_size(axis)
    return lax.all_to_all(jnp.broadcast_to(value[None], (size, *value.shape)), axis, 0, 0)


def local(
    hidden_in,
    in_gain,
    w_latent,
    q_gain,
    w_query,
    cache_keys,
    cache_values,
    lengths,
    w_out,
    post_gain,
    w_gate,
    w_up,
    w_down,
):
    n_dev = lax.axis_size(DEV)
    place = lax.axis_index(DEV).astype(jnp.int32).reshape(1)
    rows, cols = hidden_in.shape

    sums = latent_part(hidden_in, in_gain, w_latent)
    copied = {}

    def copy_query(value):
        (copied["query"],), token = ahead(value, [w_query])
        return token

    def copy_out(value):
        (copied["out"],), token = ahead(value, [w_out], D // 8 * 3)
        return token

    def copy_caches(value):
        copied["caches"], token = ahead(value, [cache_keys, cache_values])
        return token

    def copy_ffn(name, weight, value):
        (copied[name],), token = ahead(value, [weight])
        return token

    steps = n_dev.bit_length() - 1
    jobs = [copy_query] + [None] * (2 * steps - 3) + [copy_caches, copy_out]
    for name, weight in (("gate", w_gate.T), ("up", w_up.T), ("down", w_down)):
        jobs.append(functools.partial(copy_ffn, name, weight))
    jobs += [None] * (steps - 3)

    def exchanged(value, bit):
        arrived = swapped(value, DEV, bit)
        job = jobs.pop(0)
        copied["token"] = job(value) if job else copied["token"]
        return arrived, copied["token"]

    bit = 1
    while bit < n_dev:
        arrived, token = exchanged(sums, bit)
        bit *= 2
        if bit < n_dev:
            sums = joined(sums, arrived, token, True)
    query, fresh = queries(
        sums, arrived, token, q_gain, hidden_in, post_gain, copied["query"]
    )

    held, codes = query, [0]
    bit = n_dev // 2
    while bit:
        arrived, token = exchanged(held, bit)
        codes = codes + [code ^ bit for code in codes]
        bit //= 2
        if bit:
            held = joined(held, arrived, token, False)
    parts, hidden = attend(
        codes, place, lengths, token, [held, arrived], *copied["caches"]
    )
    parts = lax.all_to_all(parts, DEV, 0, 0)
    attn, sent = project(parts, query, fresh, copied["out"], w_out)

    bit = 1
    while bit < n_dev:
        arrived, token = exchanged(sent, bit)
        bit *= 2
        if bit < n_dev:
            attn, sent = summed(attn, arrived, token)
    residual, normed = normed_rows(place, attn, arrived, token, hidden)
    n_far = lax.axis_size(FAR)
    arrived = swapped(normed, FAR, 1)
    mine = joined(normed, arrived, token, False)
    other = swapped(mine, CORE, 1)
    own, other = ffn([mine, other], token, copied["gate"], copied["up"], copied["down"])

    far = lax.axis_index(FAR).astype(jnp.int32).reshape(1)
    ffn_term = combined(far, own, swapped(other, CORE, 1), n_far, n_dev)
    ffn_term = lax.all_to_all(ffn_term, (FAR, DEV), 0, 0)
    ffn_out = jnp.sum(ffn_term.astype(F32), axis=0)
    return residual + ffn_out


def solution(mesh):
    sizes = mesh.devices.shape
    mesh = jax.sharding.Mesh(
        mesh.devices.reshape(sizes[0] // 2, 2, sizes[1]), (FAR, CORE, DEV)
    )
    placed = (
        P(POOL, DEV),
        P(DEV),
        P(DEV, None),
        P(),
        P(None, DEV),
        P(POOL, DEV, None),
        P(POOL, DEV, None),
        P(POOL),
        P(DEV, None),
        P(DEV),
        P(None, (*POOL, DEV)),
        P(None, (*POOL, DEV)),
        P((*POOL, DEV), None),
    )
    return jax.shard_map(
        local, mesh=mesh, in_specs=placed, out_specs=P(POOL, DEV), check_vma=False
    )
```

```python
import functools
import math

import jax
import jax.numpy as jnp
from jax import lax
from jax.experimental import pallas as pl
from jax.experimental.pallas import tpu as pltpu
from jax.sharding import PartitionSpec as P

D = 7168
H = 64
HD = 256
QR = 2048
LATENT = QR + 2 * HD
LANES = 128
STATS = 16

EPS = 1e-05
NEG = -1e30

FAR, CORE, DEV = "far", "core", "dev"
POOL = (FAR, CORE)
F32, BF16 = jnp.float32, jnp.bfloat16
MIB = 1 << 20
VMEM = pl.BlockSpec(memory_space=pltpu.VMEM)
HBM = pl.BlockSpec(memory_space=pltpu.MemorySpace.HBM)


def dot(left, right, left_dim=1, right_dim=0):
    return lax.dot_general(
        left,
        right,
        (((left_dim,), (right_dim,)), ((), ())),
        preferred_element_type=F32,
    )


def whole(shape):
    return pl.BlockSpec(shape, lambda *_: (0,) * len(shape))


def params(mib):
    return pltpu.CompilerParams(vmem_limit_bytes=mib * MIB)


def streamed(weight):
    return pltpu.with_memory_space_constraint(weight, pltpu.MemorySpace.HBM)


def cost(flops, moved):
    return pl.CostEstimate(flops=flops, bytes_accessed=moved, transcendentals=0)


def started(source, target, sems, pieces, axis):
    width = source.shape[axis] // pieces
    copies = []
    for piece in range(pieces):
        span = pl.ds(piece * width, width)
        at = (slice(None),) * axis + (span,)
        copy = pltpu.make_async_copy(source.at[at], target.at[at], sems.at[piece])
        copy.start()
        copies.append(copy)
    return copies


def latent_kernel(hidden_ref, gain_hbm, w_hbm, out_ref, w_ref, gain_ref, sems, gain_sem):
    gain_copy = pltpu.make_async_copy(gain_hbm, gain_ref, gain_sem)
    gain_copy.start()
    copies = started(w_hbm, w_ref, sems, sems.shape[0], 1)
    hidden = hidden_ref[...].astype(F32)
    squares = jnp.sum(hidden * hidden, axis=1, keepdims=True)
    out_ref[:, LATENT:] = jnp.broadcast_to(squares, (hidden.shape[0], LANES))
    gain_copy.wait()
    scaled = (hidden * gain_ref[...][None, :]).astype(BF16)
    width = LATENT // len(copies)
    for step, copy in enumerate(copies):
        columns = slice(step * width, (step + 1) * width)
        copy.wait()
        out_ref[:, columns] = dot(scaled, w_ref[:, columns])


def latent_part(hidden, gain, w):
    rows, depth = hidden.shape
    return pl.pallas_call(
        latent_kernel,
        in_specs=[VMEM, HBM, HBM],
        out_specs=VMEM,
        out_shape=jax.ShapeDtypeStruct((rows, LATENT + LANES), F32),
        scratch_shapes=[
            pltpu.VMEM(w.shape, BF16),
            pltpu.VMEM(gain.shape, F32),
            pltpu.SemaphoreType.DMA((5,)),
            pltpu.SemaphoreType.DMA,
        ],
        compiler_params=params(8),
        cost_estimate=cost(2 * rows * depth * LATENT, 2 * depth * LATENT),
    )(hidden, streamed(gain), streamed(w))


def ahead_kernel(count, *refs):
    sources, targets = refs[1 : 1 + count], refs[1 + count : 1 + 2 * count]
    token_ref, sems = refs[-2:]
    copies = []
    for index, (source, target) in enumerate(zip(sources, targets)):
        view = source if source.shape == target.shape else source.at[:, : target.shape[1]]
        copies.append(pltpu.make_async_copy(view, target, sems.at[index]))
        copies[-1].start()
    token_ref[...] = jnp.zeros_like(token_ref)
    for copy in copies:
        copy.wait()


def ahead(beside, weights, columns=None):
    count = len(weights)
    shapes = [w.shape if columns is None else (w.shape[0], columns) for w in weights]
    *copied, token = pl.pallas_call(
        functools.partial(ahead_kernel, count),
        in_specs=[pl.BlockSpec(memory_space=pl.ANY)] + [HBM] * count,
        out_specs=[VMEM] * (count + 1),
        out_shape=[pltpu.VMEM(shape, BF16) for shape in shapes]
        + [jax.ShapeDtypeStruct((8, LANES), F32)],
        scratch_shapes=[pltpu.SemaphoreType.DMA((count,))],
        compiler_params=params(1),
        cost_estimate=cost(0, sum(2 * math.prod(shape) for shape in shapes)),
    )(beside, *[streamed(w) for w in weights])
    return copied, token


def joined(left, right, token, add):
    def kernel(left_ref, right_ref, token_ref, out_ref):
        if add:
            out_ref[...] = left_ref[...] + right_ref[...]
        else:
            both = [left_ref[...].astype(F32), right_ref[...].astype(F32)]
            out_ref[...] = jnp.concatenate(both, axis=0).astype(out_ref.dtype)

    rows, cols = left.shape
    return pl.pallas_call(
        kernel,
        in_specs=[VMEM] * 3,
        out_specs=VMEM,
        out_shape=jax.ShapeDtypeStruct((rows if add else 2 * rows, cols), left.dtype),
        compiler_params=params(2),
        cost_estimate=cost(0, 3 * rows * cols * left.dtype.itemsize),
    )(left, right, token)


def summed(value, arrived, token):
    def kernel(value_ref, arrived_ref, token_ref, out_ref, sent_ref):
        total = value_ref[...] + arrived_ref[...].astype(F32)
        out_ref[...] = total
        sent_ref[...] = total.astype(BF16)

    shape = value.shape
    return pl.pallas_call(
        kernel,
        in_specs=[VMEM] * 3,
        out_specs=[VMEM] * 2,
        out_shape=[jax.ShapeDtypeStruct(shape, F32), jax.ShapeDtypeStruct(shape, BF16)],
        compiler_params=params(2),
        cost_estimate=cost(0, 12 * math.prod(shape)),
    )(value, arrived, token)


def normed_rows(place, value, arrived, token, hidden):
    rows, n_dev = value.shape[0], hidden.shape[0]
    cols = D // n_dev

    def kernel(place_ref, value_ref, arrived_ref, token_ref, hidden_ref, own_ref, normed_ref, wide_ref):
        squares = jnp.zeros((rows, 1), F32)
        for d in range(n_dev):
            span = slice(d * cols, (d + 1) * cols)
            attn = value_ref[:, span] + arrived_ref[:, span].astype(F32)
            residual = hidden_ref[d, :rows, :cols] + attn
            wide_ref[d] = residual
            squares += jnp.sum(residual * residual, axis=1, keepdims=True)
        factor = lax.rsqrt(squares / D + EPS)
        for d in range(n_dev):
            span = slice(d * cols, (d + 1) * cols)
            scaled = wide_ref[d] * factor * hidden_ref[d, rows : rows + 1, :cols]
            normed_ref[:, span] = scaled.astype(BF16)
        own_ref[...] = wide_ref[place_ref[0]]

    return pl.pallas_call(
        kernel,
        in_specs=[pl.BlockSpec(memory_space=pltpu.SMEM)] + [VMEM] * 4,
        out_specs=[VMEM] * 2,
        out_shape=[jax.ShapeDtypeStruct((rows, cols), F32), jax.ShapeDtypeStruct((rows, D), BF16)],
        scratch_shapes=[pltpu.VMEM((n_dev, rows, cols), F32)],
        compiler_params=params(3),
        cost_estimate=cost(0, 16 * rows * D),
    )(place, value, arrived, token, hidden)


def parts_of(value):
    high = value.astype(BF16).astype(F32)
    middle = (value - high).astype(BF16).astype(F32)
    return high, middle, value - high - middle


def query_kernel(
    left_ref, right_ref, token_ref, gain_ref, hidden_ref, next_ref, w_ref, query_ref, fresh_ref, wide_ref
):
    sums_ref = left_ref[...] + right_ref[...]
    rows, cols = hidden_ref.shape
    out = w_ref.shape[1]
    width = min(512, out)
    heads = out // HD
    factor = lax.rsqrt(sums_ref[:, LATENT : LATENT + 1] / D + EPS)
    query_latent = sums_ref[:, :QR] * factor
    mean = jnp.sum(query_latent * query_latent, axis=1, keepdims=True) / QR
    normed = (query_latent * lax.rsqrt(mean + EPS) * gain_ref[...]).astype(BF16)
    fresh = sums_ref[:, QR:LATENT] * factor
    fresh_ref[...] = fresh.astype(BF16).astype(F32)
    at = rows * heads
    hidden = hidden_ref[...].astype(F32)
    wide_ref[at:, :] = jnp.zeros((wide_ref.shape[0] - at, HD), F32)
    gains = parts_of(next_ref[...][None, :])
    for first in range(0, cols, HD):
        part = min(HD, cols - first)
        wide_ref[at : at + rows, :part] = hidden[:, first : first + part]
        at += rows
    for first in range(0, cols, HD):
        part = min(HD, cols - first)
        for gain in gains:
            wide_ref[at : at + 1, :part] = gain[:, first : first + part]
            at += 1
    for step in range(out // width):
        query = dot(normed, w_ref[:, step * width : (step + 1) * width])
        for part in range(width // HD):
            head = step * (width // HD) + part
            for row in range(rows):
                wide_ref[row * heads + head : row * heads + head + 1, :] = query[
                    row : row + 1, part * HD : (part + 1) * HD
                ]
    query_ref[...] = wide_ref[...].astype(BF16)


def queries(left, right, token, gain, hidden, next_gain, w):
    rows, cols = hidden.shape
    out = w.shape[1]
    heads = out // HD
    height = -(-(rows * heads + (rows + 3) * -(-cols // HD)) // 16) * 16
    return pl.pallas_call(
        query_kernel,
        in_specs=[VMEM] * 7,
        out_specs=[VMEM] * 2,
        out_shape=[
            jax.ShapeDtypeStruct((height, HD), BF16),
            jax.ShapeDtypeStruct((rows, 2 * HD), F32),
        ],
        scratch_shapes=[pltpu.VMEM((height, HD), F32)],
        compiler_params=params(2),
        cost_estimate=cost(2 * rows * QR * out, 2 * QR * out),
    )(left, right, token, gain.reshape(1, QR), hidden, next_gain, w)


def attend_kernel(codes, place_ref, lengths_ref, token_ref, *refs):
    n_dev = len(codes)
    pieces, refs = refs[:-7], refs[-7:]
    keys_ref, values_ref, out_ref, hidden_ref, wide_ref, parts_ref, weights_ref = refs
    rows, local_pos = keys_ref.shape[:2]
    heads = H // n_dev
    height = wide_ref.shape[0] // n_dev
    me = place_ref[0]
    at = 0
    for piece in pieces:
        size = piece.shape[0]
        wide_ref[at : at + size, :] = piece[...].astype(F32)
        at += size
    blocks = hidden_ref.shape[2] // HD
    for g in range(n_dev):
        first = g * height + rows * heads
        for block in range(blocks):
            span = slice(block * HD, (block + 1) * HD)
            at = first + block * rows
            hidden_ref[me ^ codes[g], :rows, span] = wide_ref[at : at + rows, :]
            at = first + blocks * rows + 3 * block
            gain = wide_ref[at : at + 1, :] + wide_ref[at + 1 : at + 2, :]
            hidden_ref[me ^ codes[g], rows : rows + 1, span] = gain + wide_ref[at + 2 : at + 3, :]
    lane = lax.broadcasted_iota(jnp.int32, (H, LANES), 1)
    columns = lax.broadcasted_iota(jnp.int32, (H, local_pos), 1) + me * local_pos
    stats = jnp.zeros((H, LANES), F32)
    for row in range(rows):
        query = jnp.concatenate(
            [
                wide_ref[g * height + row * heads : g * height + (row + 1) * heads, :]
                for g in range(n_dev)
            ],
            axis=0,
        ).astype(BF16)
        scores = dot(query, keys_ref[row], 1, 1) * (1.0 / math.sqrt(HD))
        valid = columns < lengths_ref[row]
        masked = jnp.where(valid, scores, NEG)
        top = jnp.max(masked, axis=1, keepdims=True)
        weights = jnp.where(valid, jnp.exp(masked - top), 0.0)
        mass = jnp.sum(weights, axis=1, keepdims=True)
        weights_ref[row] = weights.astype(BF16)
        stats = jnp.where(lane == row, top, stats)
        stats = jnp.where(lane == rows + row, mass, stats)
    for row in range(rows):
        weighted = dot(weights_ref[row], values_ref[row])
        for g in range(n_dev):
            parts_ref[me ^ codes[g], row * heads : (row + 1) * heads, :] = weighted[
                g * heads : (g + 1) * heads, :
            ]
    high, middle, low = parts_of(stats)
    at = rows * heads
    parts_ref[:, at:, :] = jnp.zeros((n_dev, STATS, HD), F32)
    for g in range(n_dev):
        span = slice(g * heads, (g + 1) * heads)
        parts_ref[me ^ codes[g], at : at + heads, :LANES] = high[span]
        parts_ref[me ^ codes[g], at : at + heads, LANES:] = middle[span]
        parts_ref[me ^ codes[g], at + 8 : at + 8 + heads, :LANES] = low[span]
    out_ref[...] = parts_ref[...].astype(BF16)


def attend(codes, place, lengths, token, pieces, keys, values):
    rows, local_pos = keys.shape[:2]
    n_dev = len(codes)
    height = rows * H // n_dev + STATS
    hidden_width = -(-D // n_dev // HD) * HD
    smem = pl.BlockSpec(memory_space=pltpu.SMEM)
    return pl.pallas_call(
        functools.partial(attend_kernel, codes),
        in_specs=[smem, smem] + [VMEM] * (3 + len(pieces)),
        out_specs=[VMEM] * 2,
        out_shape=[
            jax.ShapeDtypeStruct((n_dev, height, HD), BF16),
            jax.ShapeDtypeStruct((n_dev, rows + 8, hidden_width), F32),
        ],
        scratch_shapes=[
            pltpu.VMEM((sum(piece.shape[0] for piece in pieces), HD), F32),
            pltpu.VMEM((n_dev, height, HD), F32),
            pltpu.VMEM((rows, H, local_pos), BF16),
        ],
        compiler_params=params(5),
        cost_estimate=cost(4 * rows * H * local_pos * HD, 4 * rows * local_pos * HD),
    )(place, lengths, token, *pieces, keys, values)


def project_kernel(
    sent_ref, query_ref, fresh_ref, held_ref, w_hbm, out_ref, half_ref, attended_ref, parts_ref, w_ref, sems
):
    n_dev = sent_ref.shape[0]
    held, width = held_ref.shape[1], D // 8
    copies = started(w_hbm.at[:, held:], w_ref, sems, sems.shape[0], 1)
    rows = fresh_ref.shape[0]
    heads = H // n_dev
    query = query_ref[...].astype(F32)
    parts_ref[...] = sent_ref[...].astype(F32)
    at = rows * heads
    stats = [
        parts_ref[d, at : at + heads, :LANES]
        + parts_ref[d, at : at + heads, LANES:]
        + parts_ref[d, at + 8 : at + 8 + heads, :LANES]
        for d in range(n_dev)
    ]
    for row in range(rows):
        span = slice(row * heads, (row + 1) * heads)
        key = fresh_ref[row : row + 1, :HD]
        value = fresh_ref[row : row + 1, HD:]
        score = jnp.sum(query[span] * key, axis=1, keepdims=True) * (1.0 / math.sqrt(HD))
        highest = score
        for d in range(n_dev):
            highest = jnp.maximum(highest, stats[d][:, row : row + 1])
        weight = jnp.exp(score - highest)
        mass = weight
        total = weight.astype(BF16).astype(F32) * value
        for d in range(n_dev):
            factor = jnp.exp(stats[d][:, row : row + 1] - highest)
            mass = mass + factor * stats[d][:, rows + row : rows + row + 1]
            total = total + factor * parts_ref[d, span, :]
        attended = total / mass
        for head in range(heads):
            attended_ref[row : row + 1, head * HD : (head + 1) * HD] = attended[
                head : head + 1, :
            ]

    attended = attended_ref[...].astype(BF16)
    for first in range(0, D, width):
        columns = slice(first, first + width)
        if first < held:
            total = dot(attended, held_ref[:, columns])
        else:
            copies[(first - held) // width].wait()
            total = dot(attended, w_ref[:, first - held : first - held + width])
        out_ref[:, columns] = total
        half_ref[:, columns] = total.astype(BF16)


def project(parts, query, fresh, held, w):
    rows = fresh.shape[0]
    depth = w.shape[0]
    width = D // 8
    return pl.pallas_call(
        project_kernel,
        in_specs=[VMEM] * 4 + [HBM],
        out_specs=[VMEM] * 2,
        out_shape=[jax.ShapeDtypeStruct((rows, D), F32), jax.ShapeDtypeStruct((rows, D), BF16)],
        scratch_shapes=[
            pltpu.VMEM((rows, depth), F32),
            pltpu.VMEM(parts.shape, F32),
            pltpu.VMEM((depth, D - held.shape[1]), BF16),
            pltpu.SemaphoreType.DMA(((D - held.shape[1]) // width,)),
        ],
        compiler_params=params(28),
        cost_estimate=cost(2 * rows * depth * D, 2 * depth * D),
    )(parts, query, fresh, held, streamed(w))


def ffn_kernel(*refs):
    pieces, refs = refs[:-8], refs[-8:]
    token_ref, gate_ref, up_ref, down_ref, own_ref, other_ref, sum_ref, act_ref = refs
    half, depth = own_ref.shape
    steps = 8
    width = depth // steps
    for step in range(steps):
        columns = slice(step * width, (step + 1) * width)
        rows = jnp.concatenate([piece[:, columns] for piece in pieces], axis=0)
        for weight_ref, target_ref in ((gate_ref, sum_ref), (up_ref, act_ref)):
            term = dot(weight_ref[:, columns], rows, 1, 1)
            target_ref[...] = term if step == 0 else target_ref[...] + term
    gate = sum_ref[...]
    activated = (gate / (1.0 + jnp.exp(-gate)) * act_ref[...]).T.astype(BF16)

    @pl.loop(0, steps)
    def _(step):
        columns = pl.ds(pl.multiple_of(step * width, width), width)
        term = dot(activated, down_ref[:, columns])
        own_ref[:, columns] = term[:half]
        other_ref[:, columns] = term[half:]


def ffn(pieces, token, gate_t, up_t, down):
    rows = sum(piece.shape[0] for piece in pieces)
    units, depth = gate_t.shape
    return pl.pallas_call(
        ffn_kernel,
        in_specs=[VMEM] * (len(pieces) + 4),
        out_specs=[VMEM] * 2,
        out_shape=[jax.ShapeDtypeStruct((rows // 2, depth), F32)] * 2,
        scratch_shapes=[pltpu.VMEM((units, rows), F32)] * 2,
        compiler_params=params(6),
        cost_estimate=cost(6 * rows * units * depth, 6 * units * depth),
    )(*pieces, token, gate_t, up_t, down)


def combined(far, own, arrived, n_far, n_dev):
    rows, cols = own.shape[0] // n_far, own.shape[1] // n_dev

    def kernel(far_ref, own_ref, arrived_ref, out_ref, wide_ref):
        for f in range(n_far):
            target = (far_ref[0] ^ f) * n_dev
            for d in range(n_dev):
                at = (slice(f * rows, (f + 1) * rows), slice(d * cols, (d + 1) * cols))
                wide_ref[target + d] = own_ref[at] + arrived_ref[at]
        out_ref[...] = wide_ref[...].astype(BF16)

    shape = (n_far * n_dev, rows, cols)
    return pl.pallas_call(
        kernel,
        in_specs=[pl.BlockSpec(memory_space=pltpu.SMEM)] + [VMEM] * 2,
        out_specs=VMEM,
        out_shape=jax.ShapeDtypeStruct(shape, BF16),
        scratch_shapes=[pltpu.VMEM(shape, F32)],
        compiler_params=params(4),
        cost_estimate=cost(0, 10 * math.prod(shape)),
    )(far, own, arrived)


def swapped(value, axis, bit):
    size = lax.axis_size(axis)
    return lax.ppermute(value, axis, [(i, i ^ bit) for i in range(size)])


def gathered(value, axis):
    size = lax.axis_size(axis)
    return lax.all_to_all(jnp.broadcast_to(value[None], (size, *value.shape)), axis, 0, 0)


def local(
    hidden_in,
    in_gain,
    w_latent,
    q_gain,
    w_query,
    cache_keys,
    cache_values,
    lengths,
    w_out,
    post_gain,
    w_gate,
    w_up,
    w_down,
):
    n_dev = lax.axis_size(DEV)
    place = lax.axis_index(DEV).astype(jnp.int32).reshape(1)
    rows, cols = hidden_in.shape

    sums = latent_part(hidden_in, in_gain, w_latent)
    copied = {}

    def copy_query(value):
        (copied["query"],), token = ahead(value, [w_query])
        return token

    def copy_out(value):
        (copied["out"],), token = ahead(value, [w_out], D // 8 * 3)
        return token

    def copy_caches(value):
        copied["caches"], token = ahead(value, [cache_keys, cache_values])
        return token

    def copy_ffn(name, weight, value):
        (copied[name],), token = ahead(value, [weight])
        return token

    steps = n_dev.bit_length() - 1
    jobs = [copy_query] + [None] * (2 * steps - 3) + [copy_caches, copy_out]
    for name, weight in (("gate", w_gate.T), ("up", w_up.T), ("down", w_down)):
        jobs.append(functools.partial(copy_ffn, name, weight))
    jobs += [None] * (steps - 3)

    def exchanged(value, bit):
        arrived = swapped(value, DEV, bit)
        job = jobs.pop(0)
        copied["token"] = job(value) if job else copied["token"]
        return arrived, copied["token"]

    bit = 1
    while bit < n_dev:
        arrived, token = exchanged(sums, bit)
        bit *= 2
        if bit < n_dev:
            sums = joined(sums, arrived, token, True)
    query, fresh = queries(
        sums, arrived, token, q_gain, hidden_in, post_gain, copied["query"]
    )

    held, codes = query, [0]
    bit = n_dev // 2
    while bit:
        arrived, token = exchanged(held, bit)
        codes = codes + [code ^ bit for code in codes]
        bit //= 2
        if bit:
            held = joined(held, arrived, token, False)
    parts, hidden = attend(
        codes, place, lengths, token, [held, arrived], *copied["caches"]
    )
    parts = lax.all_to_all(parts, DEV, 0, 0)
    attn, sent = project(parts, query, fresh, copied["out"], w_out)

    bit = 1
    while bit < n_dev:
        arrived, token = exchanged(sent, bit)
        bit *= 2
        if bit < n_dev:
            attn, sent = summed(attn, arrived, token)
    residual, normed = normed_rows(place, attn, arrived, token, hidden)
    n_far = lax.axis_size(FAR)
    arrived = swapped(normed, FAR, 1)
    mine = joined(normed, arrived, token, False)
    other = swapped(mine, CORE, 1)
    own, other = ffn([mine, other], token, copied["gate"], copied["up"], copied["down"])

    far = lax.axis_index(FAR).astype(jnp.int32).reshape(1)
    ffn_term = combined(far, own, swapped(other, CORE, 1), n_far, n_dev)
    ffn_term = lax.all_to_all(ffn_term, (FAR, DEV), 0, 0)
    ffn_out = jnp.sum(ffn_term.astype(F32), axis=0)
    return residual + ffn_out


def solution(mesh):
    sizes = mesh.devices.shape
    mesh = jax.sharding.Mesh(
        mesh.devices.reshape(sizes[0] // 2, 2, sizes[1]), (FAR, CORE, DEV)
    )
    placed = (
        P(POOL, DEV),
        P(DEV),
        P(DEV, None),
        P(),
        P(None, DEV),
        P(POOL, DEV, None),
        P(POOL, DEV, None),
        P(POOL),
        P(DEV, None),
        P(DEV),
        P(None, (*POOL, DEV)),
        P(None, (*POOL, DEV)),
        P((*POOL, DEV), None),
    )
    return jax.shard_map(
        local, mesh=mesh, in_specs=placed, out_specs=P(POOL, DEV), check_vma=False
    )
```
